512 devices in a mesh: ctx: 64 (over y, z), head: 4 (over x), row: 2 (over core).
Axes of the slice: x: 4, y: 8, z: 8, core: 2. Of those that a mesh axis runs over, the one named last changes fastest.
Arguments:
- hidden_states: bfloat16 [32768, 3584], P(('row', 'ctx'), 'head'), parts along dimension 0, may hold values from -40 to 40
- w_query: bfloat16 [3584, 3584], P('ctx', 'head'), may hold values from -0.09375 to 0.09375
- key_weight_matrix: bfloat16 [3584, 512], P('ctx', 'head'), may hold values from -0.09375 to 0.09375
- value_weight_matrix: bfloat16 [3584, 512], P('ctx', 'head'), may hold values from -0.09375 to 0.09375
- bias_query: float32 [3584], P('head'), may hold values from -40 to 40
- bias_key: float32 [512], P('head'), may hold values from -40 to 40
- value_bias_vector: float32 [512], P('head'), may hold values from -5 to 5
- published: int32 [128, 4], P(('row', 'ctx'), 'head'), parts along dimension 0, may hold values from 0 to 1
- vertical: int32 [128, 4, 8], P(('row', 'ctx'), 'head'), parts along dimension 0, may hold values from 0 to 62, as said below
- vcount: int32 [128, 4], P(('row', 'ctx'), 'head'), parts along dimension 0, may hold values from 0 to 8, as said below
- slash_offsets: int32 [128, 4, 16], P(('row', 'ctx'), 'head'), parts along dimension 0, may hold values from 0 to 256, as said below
- scount: int32 [128, 4], P(('row', 'ctx'), 'head'), parts along dimension 0, may hold values from 1 to 16
Outputs:
- attention: bfloat16 [32768, 3584], P(('row', 'ctx'), 'head'), parts along dimension 0
The draws below stay inside these ranges and needn't reach their ends.
There are 2 independent parts, one for each index of `row`. The reference program is written for one: setup_inputs(seed, part) draws one part's arguments, and reference() takes and returns one part's arrays. A program takes and returns all parts, laid end to end along the dimension named above; an argument that names none is the same for every part. Nothing has to cross between parts.
Inputs may be any that keep to these rules, and one draw needn't show every extreme that they name: `vertical`: for span c and head g the first vcount[c, g] entries are distinct span numbers of at most c - 1; the remaining entries are 0. vcount[c, g] is at most min(8, c); the last span's lists are full. `slash_offsets`: for span c and head g the first scount[c, g] entries are distinct; the remaining entries are 0.
All inputs are finite; a program needn't handle non-finite values.
Results may differ from the reference program's by a relative error of at most 0.007.
The reference program's roundings to bfloat16 on the way count: a program that leaves them out, or rounds other values in their place, can miss the bound.
Values may be sent and summed in bfloat16 or wider, within the bound.
A program may use at most 64 MiB of HBM per device.

```python
import jax
import jax.numpy as jnp
from jax import lax

MODEL_WIDTH = 3584
QUERY_HEADS = 28
KEY_VALUE_HEADS = 4
HEAD_SIZE = 128
SPAN_TOKENS = 256
KEY_BLOCK_TOKENS = 128
SLASH_SLOT_COUNT = 16
VERTICAL_SLOTS = 8
STRETCH_TOTAL = 64
QUERY_GROUP = 7
TOKENS = 16384


def draw_hidden_states(key, part):
    key = jax.random.fold_in(key, 1)
    normal_part = jnp.clip(jax.random.normal(key, (TOKENS, MODEL_WIDTH), jnp.float32), -5.0, 5.0)
    return normal_part.astype(jnp.bfloat16)


def draw_bias_query(key, part):
    key = jax.random.fold_in(key, 3)
    own_span_part = jnp.clip(jax.random.normal(key, (QUERY_HEADS * HEAD_SIZE,), jnp.float32), -5.0, 5.0)
    return own_span_part


def draw_bias_key(key, part):
    key = jax.random.fold_in(key, 4)
    own_span_part = jnp.clip(jax.random.normal(key, (KEY_VALUE_HEADS * HEAD_SIZE,), jnp.float32), -5.0, 5.0)
    return own_span_part


def vertical_lists(key, part):
    key = jax.random.fold_in(key, part)
    stretch_numbering = jnp.arange(STRETCH_TOTAL)
    holder_stretches = stretch_numbering[None, None, :]
    gaussian_jitter = jax.random.randint(jax.random.fold_in(key, 11), (STRETCH_TOTAL, KEY_VALUE_HEADS, STRETCH_TOTAL), 0, 4096)
    leading_position_boost = jnp.where(holder_stretches == 0, 2048, 0)
    closing_position_boost = jnp.where((holder_stretches == STRETCH_TOTAL - 2) & (stretch_numbering[:, None, None] == STRETCH_TOTAL - 1), 16384, 0)
    permitted_entries = holder_stretches <= stretch_numbering[:, None, None] - 1
    sorted_standing = jnp.where(permitted_entries, (gaussian_jitter + leading_position_boost + closing_position_boost) * STRETCH_TOTAL + holder_stretches + STRETCH_TOTAL, -1 - holder_stretches)
    ranked = lax.top_k(sorted_standing, VERTICAL_SLOTS)[1].astype(jnp.int32)
    upper_bound_index = jnp.minimum(VERTICAL_SLOTS, stretch_numbering)[:, None]
    slot_counts = jax.random.randint(jax.random.fold_in(key, 12), (STRETCH_TOTAL, KEY_VALUE_HEADS), 0, upper_bound_index + 1)
    slot_counts = jnp.where(stretch_numbering[:, None] == STRETCH_TOTAL - 1, VERTICAL_SLOTS, slot_counts).astype(jnp.int32)
    list_table = jnp.where(jnp.arange(VERTICAL_SLOTS)[None, None, :] < slot_counts[:, :, None], ranked, 0).astype(jnp.int32)
    return (list_table, slot_counts)


def draw_vertical(key, part):
    return vertical_lists(key, part)[0]


def draw_vcount(key, part):
    return vertical_lists(key, part)[1]


def slash_lists(key, part):
    key = jax.random.fold_in(key, part)
    stretch_numbering = jnp.arange(STRETCH_TOTAL)
    candidates = jnp.arange(SPAN_TOKENS)[None, None, :]
    gaussian_jitter = jax.random.randint(jax.random.fold_in(key, 31), (STRETCH_TOTAL, KEY_VALUE_HEADS, SPAN_TOKENS), 0, 65536)
    last_boost = jnp.where((candidates == SPAN_TOKENS - 1) & (stretch_numbering[:, None, None] == STRETCH_TOTAL - 1), 65536 * SPAN_TOKENS, 0)
    sorted_standing = gaussian_jitter * SPAN_TOKENS + candidates + last_boost
    ranked = (lax.top_k(sorted_standing, SLASH_SLOT_COUNT)[1] + 1).astype(jnp.int32)
    slot_counts = jax.random.randint(jax.random.fold_in(key, 32), (STRETCH_TOTAL, KEY_VALUE_HEADS), 1, SLASH_SLOT_COUNT + 1)
    slot_counts = jnp.where(stretch_numbering[:, None] == STRETCH_TOTAL - 1, SLASH_SLOT_COUNT, slot_counts).astype(jnp.int32)
    list_table = jnp.where(jnp.arange(SLASH_SLOT_COUNT)[None, None, :] < slot_counts[:, :, None], ranked, 0).astype(jnp.int32)
    return (list_table, slot_counts)


def draw_slash_offsets(key, part):
    return slash_lists(key, part)[0]


def draw_scount(key, part):
    return slash_lists(key, part)[1]


def with_ends(array, rng, least, largest):
    dims = array.shape
    spot = [jax.random.randint(jax.random.fold_in(rng, axis), (), 0, dims[axis]) for axis in range(len(dims))]
    array = array.at[tuple(spot)].set(least)
    longest = dims.index(max(dims))
    spot[longest] = (spot[longest] + 1) % dims[longest]
    return array.at[tuple(spot)].set(largest)


def block_levels(own_key, extent, cuts, smallest, high):
    def one(position, parts):
        heights = jax.random.uniform(jax.random.fold_in(jax.random.fold_in(own_key, 6), position), (parts,), jnp.float32, smallest / len(cuts), high / len(cuts))
        return jnp.repeat(jnp.exp(heights), extent[position] // parts).reshape((-1,) + (1,) * (len(extent) - position - 1))

    factor_of = one(*cuts[0])
    for cut in cuts[1:]:
        factor_of = factor_of * one(*cut)
    return factor_of


def centred(key, dims, scale, most, split=(), held_as=jnp.bfloat16):
    factor_of = block_levels(key, dims, split, -0.22, 0.18) if split else 1.0
    entries = jax.random.normal(key, dims, jnp.float32) * scale * factor_of
    return jnp.minimum(jnp.maximum(entries, -most), most).astype(held_as)


def setup_inputs(seed: int = 0, part: int = 0) -> dict:
    key_list = jax.random.split(jax.random.key(seed), 13)
    part_splits = jax.random.split(jax.random.fold_in(key_list[12], part), 13)
    hidden_states = draw_hidden_states(jax.random.fold_in(jax.random.fold_in(key_list[12], part), 71), part)
    w_query = centred(key_list[1], (MODEL_WIDTH, QUERY_HEADS * HEAD_SIZE), MODEL_WIDTH ** -0.5, 0.09375, ((0, 64), (1, 4)))
    key_weight_matrix = centred(key_list[2], (MODEL_WIDTH, KEY_VALUE_HEADS * HEAD_SIZE), MODEL_WIDTH ** -0.5, 0.09375, ((0, 64), (1, 4)))
    value_weight_matrix = centred(key_list[3], (MODEL_WIDTH, KEY_VALUE_HEADS * HEAD_SIZE), MODEL_WIDTH ** -0.5, 0.09375, ((0, 64), (1, 4)))
    bias_query = draw_bias_query(jax.random.fold_in(key_list[12], 71), part)
    bias_key = draw_bias_key(jax.random.fold_in(key_list[12], 71), part)
    value_bias_vector = centred(key_list[6], (KEY_VALUE_HEADS * HEAD_SIZE,), 1.0, 5.0, ((0, 4),), jnp.float32)
    published = with_ends(jax.random.randint(part_splits[7], (STRETCH_TOTAL, KEY_VALUE_HEADS), 0, SPAN_TOKENS // KEY_BLOCK_TOKENS), jax.random.fold_in(part_splits[7], 1), 0, (SPAN_TOKENS // KEY_BLOCK_TOKENS) - 1).astype(jnp.int32)
    vertical = draw_vertical(jax.random.fold_in(jax.random.fold_in(key_list[12], part), 71), part)
    vcount = draw_vcount(jax.random.fold_in(jax.random.fold_in(key_list[12], part), 71), part)
    slash_offsets = draw_slash_offsets(jax.random.fold_in(jax.random.fold_in(key_list[12], part), 71), part)
    scount = draw_scount(jax.random.fold_in(jax.random.fold_in(key_list[12], part), 71), part)
    return {"hidden_states": hidden_states, "w_query": w_query, "key_weight_matrix": key_weight_matrix, "value_weight_matrix": value_weight_matrix, "bias_query": bias_query, "bias_key": bias_key, "value_bias_vector": value_bias_vector, "published": published, "vertical": vertical, "vcount": vcount, "slash_offsets": slash_offsets, "scount": scount}


def frequencies(head_width):
    exponents = jnp.arange(0, head_width, 2).astype(jnp.float32) / head_width
    return jnp.power(jnp.float32(10000000.0), -exponents)


def rotate(inputs, angles):
    half_width = inputs.shape[-1] // 2
    first_half = inputs[..., :half_width]
    second_half = inputs[..., half_width:]
    cosine = jnp.cos(angles)
    sine_part = jnp.sin(angles)
    return jnp.concatenate([first_half * cosine - second_half * sine_part, second_half * cosine + first_half * sine_part], axis=-1)


def reference(hidden_states, w_query, key_weight_matrix, value_weight_matrix, bias_query, bias_key, value_bias_vector, published, vertical, vcount, slash_offsets, scount):
    score_scale = HEAD_SIZE ** -0.5
    query_rows = jnp.dot(hidden_states, w_query, preferred_element_type=jnp.float32) + bias_query
    unrotated_keys = jnp.dot(hidden_states, key_weight_matrix, preferred_element_type=jnp.float32) + bias_key
    every_value_row = (jnp.dot(hidden_states, value_weight_matrix, preferred_element_type=jnp.float32) + value_bias_vector).astype(jnp.bfloat16)
    query_rows = query_rows.reshape(STRETCH_TOTAL, SPAN_TOKENS, KEY_VALUE_HEADS, QUERY_GROUP, HEAD_SIZE)
    unrotated_keys = unrotated_keys.reshape(STRETCH_TOTAL, SPAN_TOKENS, KEY_VALUE_HEADS, HEAD_SIZE)
    every_value_row = every_value_row.reshape(STRETCH_TOTAL, SPAN_TOKENS, KEY_VALUE_HEADS, HEAD_SIZE)
    inverse = frequencies(HEAD_SIZE)
    positions = jnp.arange(SPAN_TOKENS).astype(jnp.float32)
    angle_local = positions[:, None] * inverse[None, :]
    angle_near = (positions + SPAN_TOKENS)[:, None] * inverse[None, :]
    angle_far = jnp.full((1,), 2 * SPAN_TOKENS - 1).astype(jnp.float32)[:, None] * inverse[None, :]
    rotary_keys = rotate(unrotated_keys, angle_local[None, :, None, :]).astype(jnp.bfloat16)
    query_local = rotate(query_rows, angle_local[None, :, None, None, :]).astype(jnp.bfloat16)
    query_near = rotate(query_rows, angle_near[None, :, None, None, :]).astype(jnp.bfloat16)
    query_far = rotate(query_rows, angle_far[None, :, None, None, :]).astype(jnp.bfloat16)
    key_block_count = SPAN_TOKENS // KEY_BLOCK_TOKENS
    key_block_rows = rotary_keys.reshape(STRETCH_TOTAL, key_block_count, KEY_BLOCK_TOKENS, KEY_VALUE_HEADS, HEAD_SIZE).astype(jnp.float32)
    value_block_rows = every_value_row.reshape(STRETCH_TOTAL, key_block_count, KEY_BLOCK_TOKENS, KEY_VALUE_HEADS, HEAD_SIZE).astype(jnp.float32)
    block_picker = (jnp.arange(key_block_count)[None, :, None] == published[:, None, :]).astype(jnp.float32)
    pooled_keys = jnp.einsum('cbg,cbkgd->cgkd', block_picker, key_block_rows).astype(jnp.bfloat16)
    pooled_values = jnp.einsum('cbg,cbkgd->cgkd', block_picker, value_block_rows).astype(jnp.bfloat16)
    causal = jnp.arange(SPAN_TOKENS)[:, None] >= jnp.arange(SPAN_TOKENS)[None, :]
    head_index_list = jnp.arange(KEY_VALUE_HEADS)

    def one_span(span_id):
        local_q = query_local[span_id].astype(jnp.float32)
        near_q = query_near[span_id].astype(jnp.float32)
        far_q = query_far[span_id].astype(jnp.float32)
        local_k = rotary_keys[span_id].astype(jnp.float32)
        local_v = every_value_row[span_id].astype(jnp.float32)
        before = jnp.maximum(span_id - 1, 0)
        prior_k = rotary_keys[before]
        prior_v = every_value_row[before]
        places = jnp.arange(SPAN_TOKENS)[:, None, None]
        offsets = slash_offsets[span_id]
        live_slash = jnp.arange(SLASH_SLOT_COUNT)[None, :] < scount[span_id][:, None]
        valid_near = (offsets[None] > places) & live_slash[None] & (span_id > 0)
        slash_index = jnp.where(valid_near, places - offsets[None] + SPAN_TOKENS, 0)
        near_k = prior_k[slash_index, head_index_list[None, :, None]].astype(jnp.float32)
        near_v = prior_v[slash_index, head_index_list[None, :, None]].astype(jnp.float32)
        chosen_columns = vertical[span_id]
        distant_keys = pooled_keys[chosen_columns, head_index_list[:, None]].reshape(KEY_VALUE_HEADS, VERTICAL_SLOTS * KEY_BLOCK_TOKENS, HEAD_SIZE).astype(jnp.float32)
        distant_values = pooled_values[chosen_columns, head_index_list[:, None]].reshape(KEY_VALUE_HEADS, VERTICAL_SLOTS * KEY_BLOCK_TOKENS, HEAD_SIZE).astype(jnp.float32)
        live_far = jnp.repeat(jnp.arange(VERTICAL_SLOTS)[None, :] < vcount[span_id][:, None], KEY_BLOCK_TOKENS, axis=1)
        score_local = jnp.einsum('tghd,jgd->ghtj', local_q, local_k) * score_scale
        score_local = jnp.where(causal[None, None], score_local, -jnp.inf)
        score_far = jnp.einsum('tghd,gkd->ghtk', far_q, distant_keys) * score_scale
        score_far = jnp.where(live_far[:, None, None, :], score_far, -jnp.inf)
        score_near = jnp.einsum('tghd,tgnd->ghtn', near_q, near_k) * score_scale
        score_near = jnp.where(valid_near.transpose(1, 0, 2)[:, None], score_near, -jnp.inf)
        highest = jnp.maximum(jnp.max(score_local, axis=-1, keepdims=True), jnp.maximum(jnp.max(score_far, axis=-1, keepdims=True), jnp.max(score_near, axis=-1, keepdims=True)))
        expo_local = jnp.exp(score_local - highest)
        expo_far = jnp.exp(score_far - highest)
        expo_near = jnp.exp(score_near - highest)
        totals = jnp.sum(expo_local, axis=-1, keepdims=True) + jnp.sum(expo_far, axis=-1, keepdims=True) + jnp.sum(expo_near, axis=-1, keepdims=True)
        weight_local = (expo_local / totals).astype(jnp.bfloat16).astype(jnp.float32)
        weight_far = (expo_far / totals).astype(jnp.bfloat16).astype(jnp.float32)
        weight_near = (expo_near / totals).astype(jnp.bfloat16).astype(jnp.float32)
        combined = jnp.einsum('ghtj,jgd->tghd', weight_local, local_v)
        combined = combined + jnp.einsum('ghtk,gkd->tghd', weight_far, distant_values)
        combined = combined + jnp.einsum('ghtn,tgnd->tghd', weight_near, near_v)
        return combined.astype(jnp.bfloat16)

    outputs = lax.map(one_span, jnp.arange(STRETCH_TOTAL))
    return outputs.reshape(TOKENS, QUERY_HEADS * HEAD_SIZE)
```

```python
import functools

import jax
import jax.numpy as jnp
import numpy as np
from jax import lax
from jax.experimental import pallas as pl
from jax.experimental.pallas import tpu as pltpu
from jax.sharding import PartitionSpec as P

BLOCK = 128
SIDE = 8
MASKED = -1e30
LOG2E = 1.4426950408889634
BF16, F32 = jnp.bfloat16, jnp.float32


def rope_tables(tokens, width):
    exponents = np.arange(0, width, 2).astype(np.float32) / np.float32(width)
    inverse = np.power(np.float32(10000000.0), -exponents).astype(np.float32)
    places = np.arange(tokens).astype(np.float32)

    def pair(positions):
        angles = (positions[:, None] * inverse[None, :]).astype(np.float32).astype(np.float64)
        cosine, sine = np.cos(angles), np.sin(angles)
        return [
            np.concatenate([cosine, cosine], axis=1).astype(np.float32),
            np.concatenate([-sine, sine], axis=1).astype(np.float32),
        ]

    moving = np.stack(pair(places) + pair(places + np.float32(tokens)))
    fixed = np.concatenate(pair(np.full((1,), 2 * tokens - 1, np.float32)))
    return moving, fixed


def rotate(rows, cosine, sine):
    return rows * cosine + pltpu.roll(rows, rows.shape[-1] // 2, axis=1) * sine


def kernel(
    hid, wk, wv, wq, bq, bk, bv, published, vertical, vcount, slash, scount, moving, fixed,
    out,
    hbuf, wkb, wvb, wq0, wq1, pool, kt, vv, qraw, ql, qn, qf, kft, vft,
    top1, sum1, acc1, bias_local, bias_near,
    send, recv, lsem,
):
    tokens, part = hid.shape
    width = wk.shape[1]
    group = wq.shape[1] // width
    left_cols = wq0.shape[-1]
    heads = hbuf.shape[0]
    x, c, r = lax.axis_index("head"), lax.axis_index("ctx"), lax.axis_index("row")
    y, z = c // SIDE, c % SIDE
    score_scale = width**-0.5 * LOG2E

    def at(yy, zz):
        return {"ctx": ((yy + SIDE) % SIDE) * SIDE + (zz + SIDE) % SIDE}

    sibling = {"row": 1 - r}
    x_right, x_left = {"head": (x + 1) % heads}, {"head": (x + heads - 1) % heads}
    span_next, span_prior = {"ctx": (c + 1) % SIDE**2}, {"ctx": (c + SIDE**2 - 1) % SIDE**2}

    def per_row(body):
        for rr in range(2):
            pl.when(r == rr)(functools.partial(body, rr))

    ids = {}

    def sem(*name):
        return ids.setdefault(name, len(ids))

    def copy(name, src, dst, device):
        index = sem(*name)
        return pltpu.make_async_remote_copy(
            src_ref=src,
            dst_ref=dst,
            send_sem=send.at[index],
            recv_sem=recv.at[index],
            device_id=device,
            device_id_type=pl.DeviceIdType.MESH,
        )

    class Stream:
        def __init__(self, name, bufs, share):
            self.name, self.bufs, self.share = name, bufs, share

        def slot(self, rr, i):
            return self.bufs[rr].at[y, i] if rr == 0 else self.bufs[rr].at[i, z]

        def unit(self, rr, i, sub):
            cut = pl.ds(sub * (SIDE // 2), SIDE // 2)
            return self.bufs[rr].at[i, cut] if rr == 0 else self.bufs[rr].at[cut, i]

        def row_unit(self, rr):
            return self.bufs[rr].at[y] if rr == 0 else self.bufs[rr].at[:, z]

        def first(self, rr, way, step, arriving):
            pos = z if rr == 0 else y
            i = (pos - way * (step if arriving else step - 1) + SIDE) % SIDE
            ref = self.slot(rr, i)
            device = at(y, z + way) if rr == 0 else at(y + way, z)
            return copy((self.name, "first", way, step), ref, ref, device)

        def second(self, rr, way, step, sub, arriving):
            pos = y if rr == 0 else z
            i = (pos - way * (step if arriving else step - 1) + SIDE) % SIDE
            ref = self.unit(rr, i, sub)
            device = at(y + way, z) if rr == 0 else at(y, z + way)
            return copy((self.name, "second", way, step, sub), ref, ref, device)

        def to_sibling(self, rr, way, step, sub):
            pos = y if rr == 0 else z
            if step == 0:
                ref = self.row_unit(rr)
            else:
                ref = self.unit(rr, (pos - way * step + SIDE) % SIDE, sub)
            return copy((self.name, "sibling", way, step, sub), ref, ref, sibling)

        def shared(self):
            return [(0, 0, 0)] + [(w, s, b) for w, s, b in self.seconds()]

        @staticmethod
        def firsts():
            return [(1, s) for s in (1, 2, 3, 4)] + [(-1, s) for s in (1, 2, 3)]

        @staticmethod
        def seconds():
            some = [(w, s, b) for s in (1, 2, 3) for b in (0, 1) for w in (1, -1)]
            return some + [(1, 4, 0), (-1, 4, 1)]

        def first_begin(self, rr):
            for way in (1, -1):
                self.first(rr, way, 1, False).start()

        def first_step(self, rr, step):
            for way in (1, -1):
                if (way, step) in self.firsts():
                    self.first(rr, way, step, True).wait_recv()
                    if (way, step + 1) in self.firsts():
                        self.first(rr, way, step + 1, False).start()

        def second_begin(self, rr):
            for sub in (0, 1):
                for way in (1, -1):
                    self.second(rr, way, 1, sub, False).start()
            if self.share:
                self.to_sibling(rr, 0, 0, 0).start()

        def second_step(self, rr, step, sub):
            for way in (1, -1):
                if (way, step, sub) in self.seconds():
                    self.second(rr, way, step, sub, True).wait_recv()
                    if (way, step + 1, sub) in self.seconds():
                        self.second(rr, way, step + 1, sub, False).start()
                    if self.share:
                        self.to_sibling(rr, way, step, sub).start()

        def from_sibling(self, rr):
            for way, step, sub in self.shared():
                self.to_sibling(1 - rr, way, step, sub).wait_recv()

        def finish(self, rr):
            for way, step in self.firsts():
                self.first(rr, way, step, False).wait_send()
            for way, step, sub in self.seconds():
                self.second(rr, way, step, sub, False).wait_send()
            if self.share:
                for way, step, sub in self.shared():
                    self.to_sibling(rr, way, step, sub).wait_send()

    kv_stream = Stream("kv", (wkb, wvb), True)
    q_stream = Stream("q", (wq0, wq1), True)
    pool_stream = Stream("pool", (pool, pool), False)

    own_hidden = pltpu.make_async_copy(hid, hbuf.at[x], lsem.at[0])
    own_hidden.start()

    def own_weights(rr):
        columns = pl.ds(0, left_cols) if rr == 0 else pl.ds(left_cols, wq.shape[1] - left_cols)
        return (
            pltpu.make_async_copy((wk, wv)[rr], (wkb, wvb)[rr].at[y, z], lsem.at[1]),
            pltpu.make_async_copy(wq.at[:, columns], (wq0, wq1)[rr].at[y, z], lsem.at[2]),
        )

    per_row(lambda rr: [one.start() for one in own_weights(rr)] and None)

    barrier = pltpu.get_barrier_semaphore()
    partners = (
        at(y, z + 1), at(y, z - 1), at(y + 1, z), at(y - 1, z),
        sibling, x_right, x_left, span_next, span_prior,
    )
    for device in partners:
        pl.semaphore_signal(barrier, inc=1, device_id=device, device_id_type=pl.DeviceIdType.MESH)
    pl.semaphore_wait(barrier, len(partners))

    half = tokens // 2

    def feature(way, sub, far, arriving):
        away = way * ((2 if far else 1) if arriving else (1 if far else 0))
        ref = hbuf.at[(x - away + heads) % heads, pl.ds(sub * half, half)]
        return copy(("x", way, sub, far), ref, ref, x_right if way == 1 else x_left)

    own_hidden.wait()
    for way, sub in ((1, 0), (-1, 1), (1, 1), (-1, 0)):
        feature(way, sub, False, False).start()

    def weights_begin(rr):
        first, second = own_weights(rr)
        first.wait()
        kv_stream.first_begin(rr)
        second.wait()
        q_stream.first_begin(rr)

    per_row(weights_begin)

    rows = lax.broadcasted_iota(jnp.int32, (tokens, tokens), 0)
    columns = lax.broadcasted_iota(jnp.int32, (tokens, tokens), 1)
    bias_local[...] = jnp.where(rows >= columns, 0.0, MASKED)
    back = rows - columns + tokens
    near = jnp.full((tokens, tokens), MASKED, F32)
    for e in range(slash.shape[-1]):
        offset = jnp.where((e < scount[0, 0]) & (c > 0), slash[0, 0, e], 0)
        near = jnp.where(back == offset, 0.0, near)
    bias_near[...] = near

    def weights_first(rr):
        for step in (1, 2, 3, 4):
            kv_stream.first_step(rr, step)
            if step == 4:
                kv_stream.second_begin(rr)
            q_stream.first_step(rr, step)
        q_stream.second_begin(rr)

    per_row(weights_first)
    for way, sub in ((1, 0), (-1, 1)):
        feature(way, sub, False, True).wait_recv()
        feature(way, sub, True, False).start()

    def weights_second(rr):
        for step in (1, 2, 3, 4):
            for sub in (0, 1):
                kv_stream.second_step(rr, step, sub)
        for sub in (0, 1):
            q_stream.second_step(rr, 1, sub)
        kv_stream.from_sibling(rr)

    per_row(weights_second)
    for way, sub in ((1, 1), (-1, 0)):
        feature(way, sub, False, True).wait_recv()
    for way, sub in ((1, 0), (-1, 1)):
        feature(way, sub, True, True).wait_recv()

    def project(h, weights):
        rows_of = weights.at[pl.ds(2 * h, 2)][...]
        block = rows_of.reshape(part, rows_of.shape[-1])
        return jnp.dot(hbuf[h], block, preferred_element_type=F32)

    def project_all(weights):
        total = project(0, weights)
        for h in range(1, heads):
            total = total + project(h, weights)
        return total

    keys = rotate(project_all(wkb) + bk[...], moving[0], moving[1]).astype(BF16)
    kt[0] = keys.T
    vv[0] = (project_all(wvb) + bv[...]).astype(BF16)
    behind = [
        copy(("prior", "k"), kt.at[0], kt.at[1], span_next),
        copy(("prior", "v"), vv.at[0], vv.at[1], span_next),
    ]
    for one in behind:
        one.start()
    first_block = published[0, 0] == 0
    pool[y, z, 0] = jnp.where(first_block, kt[0, :, :BLOCK], kt[0, :, BLOCK:])
    pool[y, z, 1] = jnp.where(first_block, vv[0, :BLOCK], vv[0, BLOCK:])

    def middle(rr):
        pool_stream.first_begin(rr)
        for sub in (0, 1):
            q_stream.second_step(rr, 2, sub)
        for step in (1, 2):
            pool_stream.first_step(rr, step)
        for sub in (0, 1):
            q_stream.second_step(rr, 3, sub)
        for step in (3, 4):
            pool_stream.first_step(rr, step)
        pool_stream.second_begin(rr)
        for sub in (0, 1):
            q_stream.second_step(rr, 4, sub)
        q_stream.from_sibling(rr)

    per_row(middle)

    def pool_step(step, sub):
        per_row(lambda rr: pool_stream.second_step(rr, step, sub))

    qraw[:, :left_cols] = project_all(wq0)
    pool_step(1, 0)
    qraw[:, left_cols:] = project_all(wq1)
    pool_step(1, 1)

    def rotate_head(g):
        columns = pl.ds(pl.multiple_of(g * width, width), width)
        raw = qraw[:, columns] + bq[:, columns]
        swapped = pltpu.roll(raw, width // 2, axis=1)
        ql[g] = (raw * moving[0] + swapped * moving[1]).astype(BF16)
        qn[g] = (raw * moving[2] + swapped * moving[3]).astype(BF16)
        qf[g] = (raw * fixed[0:1] + swapped * fixed[1:2]).astype(BF16)

    pl.loop(0, group)(rotate_head)
    pool_step(2, 0)
    for one in behind:
        one.wait_recv()

    def close_part(g):
        local = jnp.dot(ql[g], kt[0], preferred_element_type=F32) * score_scale + bias_local[...]
        slashed = jnp.dot(qn[g], kt[1], preferred_element_type=F32) * score_scale + bias_near[...]
        highest = jnp.maximum(
            jnp.max(local, axis=1, keepdims=True), jnp.max(slashed, axis=1, keepdims=True)
        )
        local, slashed = jnp.exp2(local - highest), jnp.exp2(slashed - highest)
        total = jnp.sum(local, axis=1, keepdims=True) + jnp.sum(slashed, axis=1, keepdims=True)
        top1[g] = jnp.broadcast_to(highest, (tokens, width))
        sum1[g] = jnp.broadcast_to(total, (tokens, width))
        acc1[g] = jnp.dot(local.astype(BF16), vv[0], preferred_element_type=F32) + jnp.dot(
            slashed.astype(BF16), vv[1], preferred_element_type=F32
        )

    for start, stop, step, sub in ((0, 2, 2, 1), (2, 4, 3, 0), (4, 6, 3, 1), (6, group, 4, 0)):
        pl.loop(start, stop)(close_part)
        pool_step(step, sub)
    pool_step(4, 1)

    slots = vertical.shape[-1]
    for e in range(slots):
        span = vertical[0, 0, e]
        kft[:, e * BLOCK : (e + 1) * BLOCK] = pool[span // SIDE, span % SIDE, 0]
        vft[e * BLOCK : (e + 1) * BLOCK] = pool[span // SIDE, span % SIDE, 1]
    place = lax.broadcasted_iota(jnp.int32, (1, slots * BLOCK), 1)
    bias_far = jnp.where(place < vcount[0, 0] * BLOCK, 0.0, MASKED)

    def far_part(g):
        scores = jnp.dot(qf[g], kft[...], preferred_element_type=F32) * score_scale + bias_far
        before = top1[g][:, :1]
        highest = jnp.maximum(before, jnp.max(scores, axis=1, keepdims=True))
        weights = jnp.exp2(scores - highest)
        fade = jnp.exp2(before - highest)
        total = sum1[g][:, :1] * fade + jnp.sum(weights, axis=1, keepdims=True)
        combined = acc1[g] * fade + jnp.dot(
            weights.astype(BF16), vft[...], preferred_element_type=F32
        )
        columns = pl.ds(pl.multiple_of(g * width, width), width)
        out[:, columns] = (combined / total).astype(BF16)

    pl.loop(0, group)(far_part)

    for way, sub in ((1, 0), (-1, 1), (1, 1), (-1, 0)):
        feature(way, sub, False, False).wait_send()
    for way, sub in ((1, 0), (-1, 1)):
        feature(way, sub, True, False).wait_send()
    for one in behind:
        one.wait_send()
    per_row(lambda rr: [s.finish(rr) for s in (kv_stream, q_stream, pool_stream)] and None)


def on_device(
    hidden_states, w_query, key_weight_matrix, value_weight_matrix, bias_query, bias_key,
    value_bias_vector, published, vertical, vcount, slash_offsets, scount,
):
    tokens, part = hidden_states.shape
    depth, width = key_weight_matrix.shape
    columns = w_query.shape[1]
    group = columns // width
    heads = lax.axis_size("head")
    slots = vertical.shape[-1]
    left = (group // 2) * width
    moving, fixed = rope_tables(tokens, width)
    hbm = pl.BlockSpec(memory_space=pl.ANY)
    vmem = pl.BlockSpec(memory_space=pltpu.VMEM)
    smem = pl.BlockSpec(memory_space=pltpu.SMEM)
    copies = 160
    return pl.pallas_call(
        kernel,
        out_shape=jax.ShapeDtypeStruct((tokens, columns), BF16),
        in_specs=[hbm] * 4 + [vmem] * 3 + [smem] * 5 + [vmem] * 2,
        out_specs=vmem,
        scratch_shapes=[
            pltpu.VMEM((heads, tokens, part), BF16),
            pltpu.VMEM((SIDE, SIDE, depth, width), BF16),
            pltpu.VMEM((SIDE, SIDE, depth, width), BF16),
            pltpu.VMEM((SIDE, SIDE, depth, left), BF16),
            pltpu.VMEM((SIDE, SIDE, depth, columns - left), BF16),
            pltpu.VMEM((SIDE, SIDE, 2, BLOCK, width), BF16),
            pltpu.VMEM((2, width, tokens), BF16),
            pltpu.VMEM((2, tokens, width), BF16),
            pltpu.VMEM((tokens, columns), F32),
            pltpu.VMEM((group, tokens, width), BF16),
            pltpu.VMEM((group, tokens, width), BF16),
            pltpu.VMEM((group, tokens, width), BF16),
            pltpu.VMEM((width, slots * BLOCK), BF16),
            pltpu.VMEM((slots * BLOCK, width), BF16),
            pltpu.VMEM((group, tokens, width), F32),
            pltpu.VMEM((group, tokens, width), F32),
            pltpu.VMEM((group, tokens, width), F32),
            pltpu.VMEM((tokens, tokens), F32),
            pltpu.VMEM((tokens, tokens), F32),
            pltpu.SemaphoreType.DMA((copies,)),
            pltpu.SemaphoreType.DMA((copies,)),
            pltpu.SemaphoreType.DMA((3,)),
        ],
        compiler_params=pltpu.CompilerParams(
            collective_id=0, has_side_effects=True, vmem_limit_bytes=56 * 1024 * 1024
        ),
        cost_estimate=pl.CostEstimate(
            flops=4 * 10**9, bytes_accessed=10**7, transcendentals=3 * 10**6
        ),
    )(
        hidden_states, key_weight_matrix, value_weight_matrix, w_query,
        bias_query.reshape(1, columns), bias_key.reshape(1, width),
        value_bias_vector.reshape(1, width),
        published, vertical, vcount, slash_offsets, scount,
        jnp.asarray(moving), jnp.asarray(fixed),
    )


def solution(mesh):
    spans, kept = P(("row", "ctx"), "head"), P(("row", "ctx"), "head", None)
    weight, bias = P("ctx", "head"), P("head")
    return jax.shard_map(
        on_device,
        mesh=mesh,
        in_specs=(spans, weight, weight, weight, bias, bias, bias, spans, kept, spans, kept, spans),
        out_specs=spans,
        check_vma=False,
    )
```

```python
import functools

import jax
import jax.numpy as jnp
import numpy as np
from jax import lax
from jax.experimental import pallas as pl
from jax.experimental.pallas import tpu as pltpu
from jax.sharding import PartitionSpec as P

BLOCK = 128
SIDE = 8
MASKED = -1e30
FIRST_ORDER = (4, 3, -3, 2, -2, 1, -1)
LOG2E = 1.4426950408889634
BF16, F32 = jnp.bfloat16, jnp.float32


def rope_tables(tokens, width):
    exponents = np.arange(0, width, 2).astype(np.float32) / np.float32(width)
    inverse = np.power(np.float32(10000000.0), -exponents).astype(np.float32)
    places = np.arange(tokens).astype(np.float32)

    def pair(positions):
        angles = (positions[:, None] * inverse[None, :]).astype(np.float32).astype(np.float64)
        cosine, sine = np.cos(angles), np.sin(angles)
        return [
            np.concatenate([cosine, cosine], axis=1).astype(np.float32),
            np.concatenate([-sine, sine], axis=1).astype(np.float32),
        ]

    moving = np.stack(pair(places) + pair(places + np.float32(tokens)))
    fixed = np.concatenate(pair(np.full((1,), 2 * tokens - 1, np.float32)))
    return moving, fixed


def rotate(rows, cosine, sine):
    return rows * cosine + pltpu.roll(rows, rows.shape[-1] // 2, axis=1) * sine


def kernel(
    hid, wk, wv, wq, bq, bk, bv, published, vertical, vcount, slash, scount, listed, moving, fixed,
    out,
    hbuf, wkb, wvb, wq0, wq1, pool, chosen, got, lists, kt, vv, qraw, ql, qn, qf, kft, vft,
    top1, sum1, acc1, bias_local, bias_near,
    send, recv, lsem,
):
    tokens, part = hid.shape
    width = wk.shape[1]
    group = wq.shape[1] // width
    left_cols = wq0.shape[-1]
    heads = hbuf.shape[0]
    slots = vertical.shape[-1]
    x, c, r = lax.axis_index("head"), lax.axis_index("ctx"), lax.axis_index("row")
    y, z = c // SIDE, c % SIDE
    score_scale = width**-0.5 * LOG2E

    def at(yy, zz):
        return {"ctx": ((yy + SIDE) % SIDE) * SIDE + (zz + SIDE) % SIDE}

    sibling = {"row": 1 - r}
    x_right, x_left = {"head": (x + 1) % heads}, {"head": (x + heads - 1) % heads}
    span_next, span_prior = {"ctx": (c + 1) % SIDE**2}, {"ctx": (c + SIDE**2 - 1) % SIDE**2}

    pos1, pos2 = jnp.where(r == 0, z, y), jnp.where(r == 0, y, z)

    def along1(d):
        there = (pos1 + d + SIDE) % SIDE
        return {"ctx": jnp.where(r == 0, y * SIDE + there, there * SIDE + z)}

    def along2(d):
        there = (pos2 + d + SIDE) % SIDE
        return {"ctx": jnp.where(r == 0, there * SIDE + z, y * SIDE + there)}

    def per_row(body):
        for rr in range(2):
            pl.when(r == rr)(functools.partial(body, rr))

    ids = {}

    def copy(name, src, dst, device):
        index = ids.setdefault(name, len(ids))
        return pltpu.make_async_remote_copy(
            src_ref=src,
            dst_ref=dst,
            send_sem=send.at[index],
            recv_sem=recv.at[index],
            device_id=device,
            device_id_type=pl.DeviceIdType.MESH,
        )

    class Weights:
        def __init__(self, name, bufs):
            self.name, self.bufs = name, bufs

        def slot(self, rr, i):
            return self.bufs[rr].at[y, i] if rr == 0 else self.bufs[rr].at[i, z]

        def unit(self, rr, away, sub=None):
            i = (pos2 + away + SIDE) % SIDE
            if sub is None:
                return self.bufs[rr].at[i] if rr == 0 else self.bufs[rr].at[:, i]
            cut = pl.ds(sub * (SIDE // 2), SIDE // 2)
            return self.bufs[rr].at[i, cut] if rr == 0 else self.bufs[rr].at[cut, i]

        def first(self, rr, d, arriving):
            ref = self.slot(rr, (pos1 - d + SIDE) % SIDE if arriving else pos1)
            return copy((self.name, "first", d), ref, ref, along1(d))

        def first_begin(self, rr):
            for d in FIRST_ORDER:
                self.first(rr, d, False).start()

        def first_end(self, rr):
            for d in reversed(FIRST_ORDER):
                self.first(rr, d, True).wait_recv()

        def second(self, rr, move, arriving):
            d, away, sub = move
            ref = self.unit(rr, away - d if arriving else away, sub)
            return copy((self.name, "second", move), ref, ref, along2(d))

        def to_sibling(self, rr, away, sub=None):
            ref = self.unit(rr, away, sub)
            return copy((self.name, "sibling", away, sub), ref, ref, sibling)

        def pass_on(self, rr, move):
            d, away, sub = move
            self.to_sibling(rr, away - d, sub).start()

        def from_sibling(self, rr):
            self.to_sibling(1 - rr, 0).wait_recv()
            for d, away, sub in self.moves:
                self.to_sibling(1 - rr, away - d, sub).wait_recv()

        def finish(self, rr):
            for d in FIRST_ORDER:
                self.first(rr, d, False).wait_send()
            self.to_sibling(rr, 0).wait_send()
            for move in self.moves:
                self.second(rr, move, False).wait_send()
                self.to_sibling(rr, move[1] - move[0], move[2]).wait_send()

    kv, query = Weights("kv", (wkb, wvb)), Weights("q", (wq0, wq1))
    kv.one = [(1, 0, None), (-1, 0, None), (2, 0, None), (-2, 0, None)]
    kv.two = [(1, -2, None), (-1, 2, None), (2, -2, 0), (-2, 2, 1)]
    kv.moves = kv.one + kv.two

    def query_move(way, step, sub):
        return (way, -way * (step - 1), sub)

    query.steps = [(w, s, b) for s in (1, 2, 3) for b in (0, 1) for w in (1, -1)]
    query.steps += [(1, SIDE // 2, 0), (-1, SIDE // 2, 1)]
    query.moves = [query_move(*step) for step in query.steps]

    def query_begin(rr):
        for step in query.steps[:4]:
            query.second(rr, query_move(*step), False).start()
        query.to_sibling(rr, 0).start()

    def query_step(rr, step, sub):
        for way in (1, -1):
            if (way, step, sub) in query.steps:
                query.second(rr, query_move(way, step, sub), True).wait_recv()
                if (way, step + 1, sub) in query.steps:
                    query.second(rr, query_move(way, step + 1, sub), False).start()
                query.pass_on(rr, query_move(way, step, sub))

    own_hidden = pltpu.make_async_copy(hid, hbuf.at[x], lsem.at[0])
    own_hidden.start()

    def own_weights(rr):
        columns = pl.ds(0, left_cols) if rr == 0 else pl.ds(left_cols, wq.shape[1] - left_cols)
        return (
            pltpu.make_async_copy((wk, wv)[rr], (wkb, wvb)[rr].at[y, z], lsem.at[1]),
            pltpu.make_async_copy(wq.at[:, columns], (wq0, wq1)[rr].at[y, z], lsem.at[2]),
        )

    per_row(lambda rr: [one.start() for one in own_weights(rr)] and None)

    barrier = pltpu.get_barrier_semaphore()
    partners = [along1(d) for d in FIRST_ORDER] + [along2(d) for d in (1, -1, 2, -2, 4)]
    partners += [sibling, x_right, x_left, span_next, span_prior]
    for device in partners:
        pl.semaphore_signal(barrier, inc=1, device_id=device, device_id_type=pl.DeviceIdType.MESH)
    pl.semaphore_wait(barrier, len(partners))

    def weights_begin(rr):
        first, second = own_weights(rr)
        first.wait()
        kv.first_begin(rr)
        second.wait()
        query.first_begin(rr)

    per_row(weights_begin)

    half = tokens // 2

    def feature(way, sub, far, arriving):
        away = way * ((2 if far else 1) if arriving else (1 if far else 0))
        ref = hbuf.at[(x - away + heads) % heads, pl.ds(sub * half, half)]
        return copy(("x", way, sub, far), ref, ref, x_right if way == 1 else x_left)

    own_hidden.wait()
    for way, sub in ((1, 0), (-1, 1), (1, 1), (-1, 0)):
        feature(way, sub, False, False).start()

    list_sends = [copy(("list", d), listed, lists.at[i], along2(d)) for i, d in ((0, -1), (1, 1))]
    for one in list_sends:
        one.start()

    rows = lax.broadcasted_iota(jnp.int32, (tokens, tokens), 0)
    columns = lax.broadcasted_iota(jnp.int32, (tokens, tokens), 1)
    bias_local[...] = jnp.where(rows >= columns, 0.0, MASKED)
    back = rows - columns + tokens
    near = jnp.full((tokens, tokens), MASKED, F32)
    for e in range(slash.shape[-1]):
        offset = jnp.where((e < scount[0, 0]) & (c > 0), slash[0, 0, e], 0)
        near = jnp.where(back == offset, 0.0, near)
    bias_near[...] = near

    def kv_first(rr):
        kv.first_end(rr)
        for move in kv.one:
            kv.second(rr, move, False).start()
        kv.to_sibling(rr, 0).start()

    per_row(kv_first)
    for way, sub in ((1, 0), (-1, 1)):
        feature(way, sub, False, True).wait_recv()
        feature(way, sub, True, False).start()

    def spread(rr):
        query.first_end(rr)
        query_begin(rr)
        for move in kv.one:
            kv.second(rr, move, True).wait_recv()
        for move in kv.two:
            kv.second(rr, move, False).start()
        for move in kv.one:
            kv.pass_on(rr, move)
        for sub in (0, 1):
            query_step(rr, 1, sub)
        for move in kv.two:
            kv.second(rr, move, True).wait_recv()
            kv.pass_on(rr, move)
        kv.from_sibling(rr)

    per_row(spread)
    for way, sub in ((1, 1), (-1, 0)):
        feature(way, sub, False, True).wait_recv()
    for way, sub in ((1, 0), (-1, 1)):
        feature(way, sub, True, True).wait_recv()

    def project(h, weights):
        rows_of = weights.at[pl.ds(2 * h, 2)][...]
        block = rows_of.reshape(part, rows_of.shape[-1])
        return jnp.dot(hbuf[h], block, preferred_element_type=F32)

    def project_all(weights):
        total = project(0, weights)
        for h in range(1, heads):
            total = total + project(h, weights)
        return total

    def query_steps(*steps):
        per_row(lambda rr: [query_step(rr, *one) for one in steps] and None)

    keys = rotate(project_all(wkb) + bk[...], moving[0], moving[1]).astype(BF16)
    kt[0] = keys.T
    query_steps((2, 0))
    vv[0] = (project_all(wvb) + bv[...]).astype(BF16)

    here = pool.at[pos1, pos2 // 2]
    first_block = published[0, 0] == 0
    here[0] = jnp.where(first_block, kt[0, :, :BLOCK], kt[0, :, BLOCK:])
    here[1] = jnp.where(first_block, vv[0, :BLOCK], vv[0, BLOCK:])

    def alike(d, arriving):
        place = (pos2 - d + SIDE) % SIDE if arriving else pos2
        ref = pool.at[pos1, place // 2]
        return copy(("alike", d), ref, ref, along2(d))

    def round_first(way, step, sub, arriving):
        i = (pos1 - way * (step if arriving else step - 1) + SIDE) % SIDE
        ref = pool.at[i, pl.ds(2 * sub, 2)]
        return copy(("round", way, step, sub), ref, ref, along1(way))

    def round_step(step, sub):
        for way in (1, -1):
            if (way, step, sub) in query.steps:
                round_first(way, step, sub, True).wait_recv()
                if (way, step + 1, sub) in query.steps:
                    round_first(way, step + 1, sub, False).start()

    for d in (4, 2, -2):
        alike(d, False).start()
    behind = [
        copy(("prior", "k"), kt.at[0], kt.at[1], span_next),
        copy(("prior", "v"), vv.at[0], vv.at[1], span_next),
    ]
    for one in behind:
        one.start()
    query_steps((2, 1), (3, 0), (3, 1))
    for d in (2, -2, 4):
        alike(d, True).wait_recv()
    for step in query.steps[:4]:
        round_first(*step, False).start()
    query_steps((4, 0), (4, 1))
    round_step(1, 0)
    per_row(query.from_sibling)

    qraw[:, :left_cols] = project_all(wq0)
    round_step(1, 1)
    qraw[:, left_cols:] = project_all(wq1)
    round_step(2, 0)

    def rotate_head(g):
        columns = pl.ds(pl.multiple_of(g * width, width), width)
        raw = qraw[:, columns] + bq[columns][None, :]
        swapped = pltpu.roll(raw, width // 2, axis=1)
        ql[g] = (raw * moving[0] + swapped * moving[1]).astype(BF16)
        qn[g] = (raw * moving[2] + swapped * moving[3]).astype(BF16)
        qf[g] = (raw * fixed[0:1] + swapped * fixed[1:2]).astype(BF16)

    pl.loop(0, 4)(rotate_head)
    round_step(2, 1)
    pl.loop(4, group)(rotate_head)
    round_step(3, 0)
    for one in behind:
        one.wait_recv()

    def close_part(g):
        local = jnp.dot(ql[g], kt[0], preferred_element_type=F32) * score_scale + bias_local[...]
        slashed = jnp.dot(qn[g], kt[1], preferred_element_type=F32) * score_scale + bias_near[...]
        highest = jnp.maximum(
            jnp.max(local, axis=1, keepdims=True), jnp.max(slashed, axis=1, keepdims=True)
        )
        local, slashed = jnp.exp2(local - highest), jnp.exp2(slashed - highest)
        total = jnp.sum(local, axis=1, keepdims=True) + jnp.sum(slashed, axis=1, keepdims=True)
        top1[g] = jnp.broadcast_to(highest, (tokens, width))
        sum1[g] = jnp.broadcast_to(total, (tokens, width))
        acc1[g] = jnp.dot(local.astype(BF16), vv[0], preferred_element_type=F32) + jnp.dot(
            slashed.astype(BF16), vv[1], preferred_element_type=F32
        )

    pl.loop(0, 1)(close_part)
    round_step(3, 1)
    pl.loop(1, 2)(close_part)
    round_step(4, 0)
    round_step(4, 1)

    def place_of(span):
        across, down = span % SIDE, span // SIDE
        return jnp.where(r == 0, across, down), jnp.where(r == 0, down, across)

    for one in list_sends:
        one.wait_recv()
    each = slots // 2
    for side in range(2):
        for e in range(each):
            one, two = place_of(lists[side, 0, side * each + e])
            chosen[side, e] = pool[one, two // 2]
    trades = [copy(("trade", d), chosen.at[i], got.at[i], along2(d)) for i, d in ((0, 1), (1, -1))]
    for one in trades:
        one.start()
    pl.loop(2, group)(close_part)
    for one in trades:
        one.wait_recv()

    for e in range(slots):
        one, two = place_of(vertical[0, 0, e])
        same = two % 2 == pos2 % 2
        block = jnp.where(same, pool[one, two // 2], got[e // each, e % each])
        kft[:, e * BLOCK : (e + 1) * BLOCK] = block[0]
        vft[e * BLOCK : (e + 1) * BLOCK] = block[1]
    place = lax.broadcasted_iota(jnp.int32, (1, slots * BLOCK), 1)
    bias_far = jnp.where(place < vcount[0, 0] * BLOCK, 0.0, MASKED)

    def far_part(g):
        scores = jnp.dot(qf[g], kft[...], preferred_element_type=F32) * score_scale + bias_far
        before = top1[g][:, :1]
        highest = jnp.maximum(before, jnp.max(scores, axis=1, keepdims=True))
        weights = jnp.exp2(scores - highest)
        fade = jnp.exp2(before - highest)
        total = sum1[g][:, :1] * fade + jnp.sum(weights, axis=1, keepdims=True)
        combined = acc1[g] * fade + jnp.dot(
            weights.astype(BF16), vft[...], preferred_element_type=F32
        )
        columns = pl.ds(pl.multiple_of(g * width, width), width)
        out[:, columns] = (combined / total).astype(BF16)

    pl.loop(0, group)(far_part)

    for way, sub in ((1, 0), (-1, 1), (1, 1), (-1, 0)):
        feature(way, sub, False, False).wait_send()
    for way, sub in ((1, 0), (-1, 1)):
        feature(way, sub, True, False).wait_send()
    for one in behind + trades + list_sends:
        one.wait_send()
    for d in (4, 2, -2):
        alike(d, False).wait_send()
    for step in query.steps:
        round_first(*step, False).wait_send()
    per_row(lambda rr: [one.finish(rr) for one in (kv, query)] and None)


def on_device(
    hidden_states, w_query, key_weight_matrix, value_weight_matrix, bias_query, bias_key,
    value_bias_vector, published, vertical, vcount, slash_offsets, scount,
):
    tokens, part = hidden_states.shape
    depth, width = key_weight_matrix.shape
    columns = w_query.shape[1]
    group = columns // width
    heads = lax.axis_size("head")
    slots = vertical.shape[-1]
    left = (group // 2) * width
    moving, fixed = rope_tables(tokens, width)
    hbm = pl.BlockSpec(memory_space=pl.ANY)
    vmem = pl.BlockSpec(memory_space=pltpu.VMEM)
    smem = pl.BlockSpec(memory_space=pltpu.SMEM)
    copies = 160
    return pl.pallas_call(
        kernel,
        out_shape=jax.ShapeDtypeStruct((tokens, columns), BF16),
        in_specs=[hbm] * 4 + [vmem] * 3 + [smem] * 5 + [hbm] + [vmem] * 2,
        out_specs=vmem,
        scratch_shapes=[
            pltpu.VMEM((heads, tokens, part), BF16),
            pltpu.VMEM((SIDE, SIDE, depth, width), BF16),
            pltpu.VMEM((SIDE, SIDE, depth, width), BF16),
            pltpu.VMEM((SIDE, SIDE, depth, left), BF16),
            pltpu.VMEM((SIDE, SIDE, depth, columns - left), BF16),
            pltpu.VMEM((SIDE, SIDE // 2, 2, BLOCK, width), BF16),
            pltpu.VMEM((2, slots // 2, 2, BLOCK, width), BF16),
            pltpu.VMEM((2, slots // 2, 2, BLOCK, width), BF16),
            pltpu.SMEM((2, 1, slots), jnp.int32),
            pltpu.VMEM((2, width, tokens), BF16),
            pltpu.VMEM((2, tokens, width), BF16),
            pltpu.VMEM((tokens, columns), F32),
            pltpu.VMEM((group, tokens, width), BF16),
            pltpu.VMEM((group, tokens, width), BF16),
            pltpu.VMEM((group, tokens, width), BF16),
            pltpu.VMEM((width, slots * BLOCK), BF16),
            pltpu.VMEM((slots * BLOCK, width), BF16),
            pltpu.VMEM((group, tokens, width), F32),
            pltpu.VMEM((group, tokens, width), F32),
            pltpu.VMEM((group, tokens, width), F32),
            pltpu.VMEM((tokens, tokens), F32),
            pltpu.VMEM((tokens, tokens), F32),
            pltpu.SemaphoreType.DMA((copies,)),
            pltpu.SemaphoreType.DMA((copies,)),
            pltpu.SemaphoreType.DMA((3,)),
        ],
        compiler_params=pltpu.CompilerParams(
            collective_id=0, has_side_effects=True, vmem_limit_bytes=56 * 1024 * 1024
        ),
        cost_estimate=pl.CostEstimate(
            flops=4 * 10**9, bytes_accessed=10**7, transcendentals=3 * 10**6
        ),
    )(
        hidden_states, key_weight_matrix, value_weight_matrix, w_query,
        bias_query, bias_key.reshape(1, width),
        value_bias_vector.reshape(1, width),
        published, vertical, vcount, slash_offsets, scount,
        vertical[0], jnp.asarray(moving), jnp.asarray(fixed),
    )


def solution(mesh):
    spans, kept = P(("row", "ctx"), "head"), P(("row", "ctx"), "head", None)
    weight, bias = P("ctx", "head"), P("head")
    return jax.shard_map(
        on_device,
        mesh=mesh,
        in_specs=(spans, weight, weight, weight, bias, bias, bias, spans, kept, spans, kept, spans),
        out_specs=spans,
        check_vma=False,
    )
```

```python
import functools

import jax
import jax.numpy as jnp
import numpy as np
from jax import lax
from jax.experimental import pallas as pl
from jax.experimental.pallas import tpu as pltpu
from jax.sharding import PartitionSpec as P

BLOCK = 128
SIDE = 8
MASKED = -1e30
FIRST_ORDER = (4, 3, -3, 2, -2, 1, -1)
LOG2E = 1.4426950408889634
BF16, F32 = jnp.bfloat16, jnp.float32


def rope_tables(tokens, width):
    exponents = np.arange(0, width, 2).astype(np.float32) / np.float32(width)
    inverse = np.power(np.float32(10000000.0), -exponents).astype(np.float32)
    places = np.arange(tokens).astype(np.float32)

    def pair(positions):
        angles = (positions[:, None] * inverse[None, :]).astype(np.float32).astype(np.float64)
        cosine, sine = np.cos(angles), np.sin(angles)
        return [
            np.concatenate([cosine, cosine], axis=1).astype(np.float32),
            np.concatenate([-sine, sine], axis=1).astype(np.float32),
        ]

    moving = np.stack(pair(places) + pair(places + np.float32(tokens)))
    fixed = np.concatenate(pair(np.full((1,), 2 * tokens - 1, np.float32)))
    return moving, fixed


def rotate(rows, cosine, sine):
    return rows * cosine + pltpu.roll(rows, rows.shape[-1] // 2, axis=1) * sine


def kernel(
    hid, wk, wv, wq, moving_hbm, published_hbm, vertical_hbm, vcount_hbm, slash_hbm, scount_hbm,
    bq, bk, bv, fixed,
    out_hbm,
    out, moving, published, vertical, vcount, slash, scount, hbuf, wkb, wvb, wq0, wq1, pool, chosen, got, lists, kt, vv, qraw, ql, qn, qf, kft, vft,
    top1, sum1, acc1, bias_local, bias_near,
    send, recv, lsem, osem,
):
    tokens, part = hid.shape
    width = wk.shape[1]
    group = wq.shape[1] // width
    left_cols = wq0.shape[-1]
    heads = hbuf.shape[0]
    slots = vertical.shape[-1]
    x, c, r = lax.axis_index("head"), lax.axis_index("ctx"), lax.axis_index("row")
    y, z = c // SIDE, c % SIDE
    score_scale = width**-0.5 * LOG2E

    def at(yy, zz):
        return {"ctx": ((yy + SIDE) % SIDE) * SIDE + (zz + SIDE) % SIDE}

    sibling = {"row": 1 - r}
    x_right, x_left = {"head": (x + 1) % heads}, {"head": (x + heads - 1) % heads}
    span_next, span_prior = {"ctx": (c + 1) % SIDE**2}, {"ctx": (c + SIDE**2 - 1) % SIDE**2}

    pos1, pos2 = jnp.where(r == 0, z, y), jnp.where(r == 0, y, z)

    def along1(d):
        there = (pos1 + d + SIDE) % SIDE
        return {"ctx": jnp.where(r == 0, y * SIDE + there, there * SIDE + z)}

    def along2(d):
        there = (pos2 + d + SIDE) % SIDE
        return {"ctx": jnp.where(r == 0, there * SIDE + z, y * SIDE + there)}

    def per_row(body):
        for rr in range(2):
            pl.when(r == rr)(functools.partial(body, rr))

    ids = {}

    def copy(name, src, dst, device):
        index = ids.setdefault(name, len(ids))
        return pltpu.make_async_remote_copy(
            src_ref=src,
            dst_ref=dst,
            send_sem=send.at[index],
            recv_sem=recv.at[index],
            device_id=device,
            device_id_type=pl.DeviceIdType.MESH,
        )

    class Weights:
        def __init__(self, name, bufs):
            self.name, self.bufs = name, bufs

        def slot(self, rr, i):
            return self.bufs[rr].at[y, i] if rr == 0 else self.bufs[rr].at[i, z]

        def unit(self, rr, away, sub=None):
            i = (pos2 + away + SIDE) % SIDE
            if sub is None:
                return self.bufs[rr].at[i] if rr == 0 else self.bufs[rr].at[:, i]
            cut = pl.ds(sub * (SIDE // 2), SIDE // 2)
            return self.bufs[rr].at[i, cut] if rr == 0 else self.bufs[rr].at[cut, i]

        def first(self, rr, move, arriving):
            d, away = move
            ref = self.slot(rr, (pos1 + (away - d if arriving else away) + SIDE) % SIDE)
            return copy((self.name, "first", move), ref, ref, along1(d))

        def first_begin(self, rr, moves):
            for move in moves:
                self.first(rr, move, False).start()

        def first_end(self, rr, moves):
            for move in reversed(moves):
                self.first(rr, move, True).wait_recv()

        def second(self, rr, move, arriving):
            d, away, sub = move
            ref = self.unit(rr, away - d if arriving else away, sub)
            return copy((self.name, "second", move), ref, ref, along2(d))

        def to_sibling(self, rr, away, sub=None):
            ref = self.unit(rr, away, sub)
            return copy((self.name, "sibling", away, sub), ref, ref, sibling)

        def pass_on(self, rr, move):
            d, away, sub = move
            self.to_sibling(rr, away - d, sub).start()

        def from_sibling(self, rr):
            self.to_sibling(1 - rr, 0).wait_recv()
            for d, away, sub in self.moves:
                self.to_sibling(1 - rr, away - d, sub).wait_recv()

        def finish(self, rr):
            for move in self.near + self.far:
                self.first(rr, move, False).wait_send()
            self.to_sibling(rr, 0).wait_send()
            for move in self.moves:
                self.second(rr, move, False).wait_send()
                self.to_sibling(rr, move[1] - move[0], move[2]).wait_send()

    kv, query = Weights("kv", (wkb, wvb)), Weights("q", (wq0, wq1))
    kv.near, kv.far = [(d, 0) for d in FIRST_ORDER], []
    query.near, query.far = [(2, 0), (-2, 0), (1, 0), (-1, 0)], [(2, -2), (1, -2), (-1, 2)]
    kv.one = [(1, 0, None), (-1, 0, None), (2, 0, None), (-2, 0, None)]
    kv.two = [(1, -2, None), (-1, 2, None), (2, -2, 0), (-2, 2, 1)]
    kv.moves = kv.one + kv.two

    def query_move(way, step, sub):
        return (way, -way * (step - 1), sub)

    query.steps = [(w, s, b) for s in (1, 2, 3) for b in (0, 1) for w in (1, -1)]
    query.steps += [(1, SIDE // 2, 0), (-1, SIDE // 2, 1)]
    query.moves = [query_move(*step) for step in query.steps]

    def query_begin(rr, sub):
        for way in (1, -1):
            query.second(rr, query_move(way, 1, sub), False).start()

    def query_step(rr, step, sub):
        for way in (1, -1):
            if (way, step, sub) in query.steps:
                query.second(rr, query_move(way, step, sub), True).wait_recv()
                if (way, step + 1, sub) in query.steps:
                    query.second(rr, query_move(way, step + 1, sub), False).start()
                query.pass_on(rr, query_move(way, step, sub))

    own_hidden = pltpu.make_async_copy(hid, hbuf.at[x], lsem.at[0])
    own_hidden.start()
    tables = pltpu.make_async_copy(moving_hbm, moving, lsem.at[3])
    tables.start()
    small = [
        pltpu.make_async_copy(src, dst, lsem.at[4 + i])
        for i, (src, dst) in enumerate(
            (
                (published_hbm, published),
                (vertical_hbm, vertical),
                (vcount_hbm, vcount),
                (slash_hbm, slash),
                (scount_hbm, scount),
            )
        )
    ]
    for one in small:
        one.start()

    def own_weights(rr):
        columns = pl.ds(0, left_cols) if rr == 0 else pl.ds(left_cols, wq.shape[1] - left_cols)
        return (
            pltpu.make_async_copy((wk, wv)[rr], (wkb, wvb)[rr].at[y, z], lsem.at[1]),
            pltpu.make_async_copy(wq.at[:, columns], (wq0, wq1)[rr].at[y, z], lsem.at[2]),
        )

    per_row(lambda rr: [one.start() for one in own_weights(rr)] and None)

    barrier = pltpu.get_barrier_semaphore()
    partners = [along1(d) for d in FIRST_ORDER] + [along2(d) for d in (1, -1, 2, -2, 4)]
    partners += [sibling, x_right, x_left, span_next, span_prior]
    for device in partners:
        pl.semaphore_signal(barrier, inc=1, device_id=device, device_id_type=pl.DeviceIdType.MESH)
    pl.semaphore_wait(barrier, len(partners))

    def weights_begin(rr):
        first, second = own_weights(rr)
        first.wait()
        kv.first_begin(rr, kv.near)
        second.wait()
        query.first_begin(rr, query.near)

    per_row(weights_begin)

    half = tokens // 2

    def feature(way, sub, far, arriving):
        away = way * ((2 if far else 1) if arriving else (1 if far else 0))
        ref = hbuf.at[(x - away + heads) % heads, pl.ds(sub * half, half)]
        return copy(("x", way, sub, far), ref, ref, x_right if way == 1 else x_left)

    own_hidden.wait()
    for way, sub in ((1, 0), (-1, 1), (1, 1), (-1, 0)):
        feature(way, sub, False, False).start()

    list_sends = [copy(("list", d), vertical_hbm.at[0], lists.at[i], along2(d)) for i, d in ((0, -1), (1, 1))]
    for one in list_sends:
        one.start()

    for one in small:
        one.wait()
    tables.wait()

    rows = lax.broadcasted_iota(jnp.int32, (tokens, tokens), 0)
    columns = lax.broadcasted_iota(jnp.int32, (tokens, tokens), 1)
    bias_local[...] = jnp.where(rows >= columns, 0.0, MASKED)
    back = rows - columns + tokens
    near = jnp.full((tokens, tokens), MASKED, F32)
    for e in range(slash.shape[-1]):
        offset = jnp.where((e < scount[0, 0]) & (c > 0), slash[0, 0, e], 0)
        near = jnp.where(back == offset, 0.0, near)
    bias_near[...] = near

    def kv_first(rr):
        kv.first_end(rr, kv.near)
        for move in kv.one:
            kv.second(rr, move, False).start()
        kv.to_sibling(rr, 0).start()
        query.first_end(rr, query.near)
        query.first_begin(rr, query.far)

    per_row(kv_first)
    for way, sub in ((1, 0), (-1, 1)):
        feature(way, sub, False, True).wait_recv()
        feature(way, sub, True, False).start()

    def spread(rr):
        query.first_end(rr, query.far)
        query_begin(rr, 0)
        for move in kv.one:
            kv.second(rr, move, True).wait_recv()
        for move in kv.two:
            kv.second(rr, move, False).start()
        query_begin(rr, 1)
        for move in kv.one:
            kv.pass_on(rr, move)
        query.to_sibling(rr, 0).start()
        query_step(rr, 1, 0)
        for move in kv.two:
            kv.second(rr, move, True).wait_recv()
            kv.pass_on(rr, move)
        query_step(rr, 1, 1)
        kv.from_sibling(rr)

    per_row(spread)
    for way, sub in ((1, 1), (-1, 0)):
        feature(way, sub, False, True).wait_recv()
    for way, sub in ((1, 0), (-1, 1)):
        feature(way, sub, True, True).wait_recv()

    def project(h, *weights):
        parts = [one.at[pl.ds(2 * h, 2)][...] for one in weights]
        block = jnp.concatenate([one.reshape(part, one.shape[-1]) for one in parts], axis=1)
        return jnp.dot(hbuf[h], block, preferred_element_type=F32)

    def project_all(*weights):
        total = project(0, *weights)
        for h in range(1, heads):
            total = total + project(h, *weights)
        return total

    def query_steps(*steps):
        per_row(lambda rr: [query_step(rr, *one) for one in steps] and None)

    both = project_all(wkb, wvb)
    keys = rotate(both[:, :width] + bk[...][None, :], moving[0], moving[1]).astype(BF16)
    kt[0] = keys.T
    vv[0] = (both[:, width:] + bv[...][None, :]).astype(BF16)

    here = pool.at[pos1, pos2 // 2]
    first_block = published[0, 0] == 0
    here[0] = jnp.where(first_block, kt[0, :, :BLOCK], kt[0, :, BLOCK:])
    here[1] = jnp.where(first_block, vv[0, :BLOCK], vv[0, BLOCK:])

    def alike(d, arriving):
        place = (pos2 - d + SIDE) % SIDE if arriving else pos2
        ref = pool.at[pos1, place // 2]
        return copy(("alike", d), ref, ref, along2(d))

    offsets = (0, 2, -2, 4)

    def around(way, step, o, arriving):
        i = (pos1 - way * (step if arriving else step - 1) + SIDE) % SIDE
        ref = pool.at[i, (pos2 + o + SIDE) % SIDE // 2]
        return copy(("round", way, step, o), ref, ref, along1(way))

    def ways(step, o):
        return (1, -1) if step < SIDE // 2 else (1,) if o in (0, 2) else (-1,)

    def round_begin(o):
        for way in (1, -1):
            around(way, 1, o, False).start()

    def round_step(step, o):
        for way in ways(step, o):
            around(way, step, o, True).wait_recv()
            if step < SIDE // 2 and way in ways(step + 1, o):
                around(way, step + 1, o, False).start()

    for d in (2, -2, 4):
        alike(d, False).start()
    round_begin(0)
    query_steps((2, 0), (2, 1))
    round_step(1, 0)
    for d in (2, -2):
        alike(d, True).wait_recv()
        round_begin(-d)
    query_steps((3, 0))
    alike(4, True).wait_recv()
    round_begin(4)
    round_step(2, 0)
    round_step(1, 2)
    round_step(1, -2)
    query_steps((3, 1))
    round_step(1, 4)
    round_step(3, 0)
    round_step(2, 2)
    round_step(2, -2)
    query_steps((4, 0), (4, 1))
    round_step(2, 4)
    round_step(4, 0)
    round_step(3, 2)
    round_step(3, -2)
    behind = [
        copy(("prior", "k"), kt.at[0], kt.at[1], span_next),
        copy(("prior", "v"), vv.at[0], vv.at[1], span_next),
    ]
    for one in behind:
        one.start()
    per_row(query.from_sibling)

    qraw[:, :left_cols] = project_all(wq0)
    round_step(3, 4)
    qraw[:, left_cols:] = project_all(wq1)

    def rotate_head(g):
        columns = pl.ds(pl.multiple_of(g * width, width), width)
        raw = qraw[:, columns] + bq[columns][None, :]
        swapped = pltpu.roll(raw, width // 2, axis=1)
        ql[g] = (raw * moving[0] + swapped * moving[1]).astype(BF16)
        qn[g] = (raw * moving[2] + swapped * moving[3]).astype(BF16)
        qf[g] = (raw * fixed[0:1] + swapped * fixed[1:2]).astype(BF16)

    pl.loop(0, 4)(rotate_head)
    round_step(4, 2)
    round_step(4, -2)
    pl.loop(4, group)(rotate_head)
    for one in behind:
        one.wait_recv()

    def close_part(g):
        local = jnp.dot(ql[g], kt[0], preferred_element_type=F32) * score_scale + bias_local[...]
        slashed = jnp.dot(qn[g], kt[1], preferred_element_type=F32) * score_scale + bias_near[...]
        highest = jnp.maximum(
            jnp.max(local, axis=1, keepdims=True), jnp.max(slashed, axis=1, keepdims=True)
        )
        local, slashed = jnp.exp2(local - highest), jnp.exp2(slashed - highest)
        total = jnp.sum(local, axis=1, keepdims=True) + jnp.sum(slashed, axis=1, keepdims=True)
        top1[g] = jnp.broadcast_to(highest, (tokens, width))
        sum1[g] = jnp.broadcast_to(total, (tokens, width))
        acc1[g] = jnp.dot(local.astype(BF16), vv[0], preferred_element_type=F32) + jnp.dot(
            slashed.astype(BF16), vv[1], preferred_element_type=F32
        )

    pl.loop(0, 1)(close_part)
    round_step(4, 4)

    def place_of(span):
        across, down = span % SIDE, span // SIDE
        return jnp.where(r == 0, across, down), jnp.where(r == 0, down, across)

    for one in list_sends:
        one.wait_recv()
    each = slots // 2
    trades = {}
    for which in range(2):
        for side, d in ((0, 1), (1, -1)):
            for e in range(each):
                one, two = place_of(lists[side, 0, side * each + e])
                chosen[side, which, e] = pool[one, two // 2, which]
            src, dst = chosen.at[side, which], got.at[side, which]
            trades[side, which] = copy(("trade", d, which), src, dst, along2(d))
            trades[side, which].start()
    pl.loop(1, group)(close_part)

    def listed(e, which):
        one, two = place_of(vertical[0, 0, e])
        traded = got[e // each, which, e % each]
        return jnp.where(two % 2 == pos2 % 2, pool[one, two // 2, which], traded)

    for side in range(2):
        trades[side, 0].wait_recv()
    for e in range(slots):
        kft[:, e * BLOCK : (e + 1) * BLOCK] = listed(e, 0)
    place = lax.broadcasted_iota(jnp.int32, (1, slots * BLOCK), 1)
    bias_far = jnp.where(place < vcount[0, 0] * BLOCK, 0.0, MASKED)

    def far_scores(g):
        return jnp.dot(qf[g], kft[...], preferred_element_type=F32) * score_scale + bias_far

    def far_part(g, scores):
        before = top1[g][:, :1]
        highest = jnp.maximum(before, jnp.max(scores, axis=1, keepdims=True))
        weights = jnp.exp2(scores - highest)
        fade = jnp.exp2(before - highest)
        total = sum1[g][:, :1] * fade + jnp.sum(weights, axis=1, keepdims=True)
        combined = acc1[g] * fade + jnp.dot(
            weights.astype(BF16), vft[...], preferred_element_type=F32
        )
        columns = pl.ds(g * width, width)
        out[:, columns] = (combined / total).astype(BF16)
        pltpu.make_async_copy(out.at[:, columns], out_hbm.at[:, columns], osem.at[g]).start()

    scores = far_scores(0)
    for side in range(2):
        trades[side, 1].wait_recv()
    for e in range(slots):
        vft[e * BLOCK : (e + 1) * BLOCK] = listed(e, 1)
    for g in range(group):
        far_part(g, scores)
        if g + 1 < group:
            scores = far_scores(g + 1)

    for way, sub in ((1, 0), (-1, 1), (1, 1), (-1, 0)):
        feature(way, sub, False, False).wait_send()
    for way, sub in ((1, 0), (-1, 1)):
        feature(way, sub, True, False).wait_send()
    for one in behind + list(trades.values()) + list_sends:
        one.wait_send()
    for d in (4, 2, -2):
        alike(d, False).wait_send()
    for o in offsets:
        for step in (1, 2, 3, 4):
            for way in ways(step, o):
                around(way, step, o, False).wait_send()
    per_row(lambda rr: [one.finish(rr) for one in (kv, query)] and None)
    for g in range(group):
        columns = pl.ds(g * width, width)
        pltpu.make_async_copy(out.at[:, columns], out_hbm.at[:, columns], osem.at[g]).wait()


def on_device(
    hidden_states, w_query, key_weight_matrix, value_weight_matrix, bias_query, bias_key,
    value_bias_vector, published, vertical, vcount, slash_offsets, scount,
):
    tokens, part = hidden_states.shape
    depth, width = key_weight_matrix.shape
    columns = w_query.shape[1]
    group = columns // width
    heads = lax.axis_size("head")
    slots = vertical.shape[-1]
    left = (group // 2) * width
    moving, fixed = rope_tables(tokens, width)
    hbm = pl.BlockSpec(memory_space=pl.ANY)
    vmem = pl.BlockSpec(memory_space=pltpu.VMEM)
    copies = 160
    return pl.pallas_call(
        kernel,
        out_shape=jax.ShapeDtypeStruct((tokens, columns), BF16),
        in_specs=[hbm] * 10 + [vmem] * 4,
        out_specs=hbm,
        scratch_shapes=[
            pltpu.VMEM((tokens, columns), BF16),
            pltpu.VMEM(moving.shape, F32),
            pltpu.SMEM(published.shape, jnp.int32),
            pltpu.SMEM(vertical.shape, jnp.int32),
            pltpu.SMEM(vcount.shape, jnp.int32),
            pltpu.SMEM(slash_offsets.shape, jnp.int32),
            pltpu.SMEM(scount.shape, jnp.int32),
            pltpu.VMEM((heads, tokens, part), BF16),
            pltpu.VMEM((SIDE, SIDE, depth, width), BF16),
            pltpu.VMEM((SIDE, SIDE, depth, width), BF16),
            pltpu.VMEM((SIDE, SIDE, depth, left), BF16),
            pltpu.VMEM((SIDE, SIDE, depth, columns - left), BF16),
            pltpu.VMEM((SIDE, SIDE // 2, 2, BLOCK, width), BF16),
            pltpu.VMEM((2, 2, slots // 2, BLOCK, width), BF16),
            pltpu.VMEM((2, 2, slots // 2, BLOCK, width), BF16),
            pltpu.SMEM((2, 1, slots), jnp.int32),
            pltpu.VMEM((2, width, tokens), BF16),
            pltpu.VMEM((2, tokens, width), BF16),
            pltpu.VMEM((tokens, columns), F32),
            pltpu.VMEM((group, tokens, width), BF16),
            pltpu.VMEM((group, tokens, width), BF16),
            pltpu.VMEM((group, tokens, width), BF16),
            pltpu.VMEM((width, slots * BLOCK), BF16),
            pltpu.VMEM((slots * BLOCK, width), BF16),
            pltpu.VMEM((group, tokens, width), F32),
            pltpu.VMEM((group, tokens, width), F32),
            pltpu.VMEM((group, tokens, width), F32),
            pltpu.VMEM((tokens, tokens), F32),
            pltpu.VMEM((tokens, tokens), F32),
            pltpu.SemaphoreType.DMA((copies,)),
            pltpu.SemaphoreType.DMA((copies,)),
            pltpu.SemaphoreType.DMA((9,)),
            pltpu.SemaphoreType.DMA((group,)),
        ],
        compiler_params=pltpu.CompilerParams(
            collective_id=0, has_side_effects=True, vmem_limit_bytes=56 * 1024 * 1024
        ),
        cost_estimate=pl.CostEstimate(
            flops=4 * 10**9, bytes_accessed=10**7, transcendentals=3 * 10**6
        ),
    )(
        hidden_states, key_weight_matrix, value_weight_matrix, w_query, jnp.asarray(moving),
        published, vertical, vcount, slash_offsets, scount,
        bias_query, bias_key, value_bias_vector, jnp.asarray(fixed),
    )


def solution(mesh):
    spans, kept = P(("row", "ctx"), "head"), P(("row", "ctx"), "head", None)
    weight, bias = P("ctx", "head"), P("head")
    return jax.shard_map(
        on_device,
        mesh=mesh,
        in_specs=(spans, weight, weight, weight, bias, bias, bias, spans, kept, spans, kept, spans),
        out_specs=spans,
        check_vma=False,
    )
```

```python
import functools

import jax
import jax.numpy as jnp
import numpy as np
from jax import lax
from jax.experimental import pallas as pl
from jax.experimental.pallas import tpu as pltpu
from jax.sharding import PartitionSpec as P

BLOCK = 128
SIDE = 8
MASKED = -1e30
FIRST_ORDER = (4, 3, -3, 2, -2, 1, -1)
REACH = 2
LOG2E = 1.4426950408889634
BF16, F32 = jnp.bfloat16, jnp.float32


def rope_tables(tokens, width):
    exponents = np.arange(0, width, 2).astype(np.float32) / np.float32(width)
    inverse = np.power(np.float32(10000000.0), -exponents).astype(np.float32)
    places = np.arange(tokens).astype(np.float32)

    def pair(positions):
        angles = (positions[:, None] * inverse[None, :]).astype(np.float32).astype(np.float64)
        cosine, sine = np.cos(angles), np.sin(angles)
        return [
            np.concatenate([cosine, cosine], axis=1).astype(np.float32),
            np.concatenate([-sine, sine], axis=1).astype(np.float32),
        ]

    moving = np.stack(pair(places) + pair(places + np.float32(tokens)))
    fixed = np.concatenate(pair(np.full((1,), 2 * tokens - 1, np.float32)))
    return moving, fixed


def rotate(rows, cosine, sine):
    return rows * cosine + pltpu.roll(rows, rows.shape[-1] // 2, axis=1) * sine


def kernel(
    hid, wk, wv, wq, moving_hbm, published_hbm, vertical_hbm, vcount_hbm, slash_hbm, scount_hbm,
    bq, bk, bv, fixed,
    out,
    moving, published, vertical, vcount, slash, scount, hbuf, wkb, wvb, wq0, wq1, pool, chosen, got, lists, kt, vv, qraw, ql, qn, qf, kft, vft,
    top1, sum1, acc1, bias_local, bias_near,
    send, recv, lsem, osem,
):
    tokens, part = hid.shape
    width = wk.shape[1]
    group = wq.shape[1] // width
    left_cols = wq0.shape[-1]
    heads = hbuf.shape[0]
    slots = vertical.shape[-1]
    x, c, r = lax.axis_index("head"), lax.axis_index("ctx"), lax.axis_index("row")
    y, z = c // SIDE, c % SIDE
    score_scale = width**-0.5 * LOG2E

    def at(yy, zz):
        return {"ctx": ((yy + SIDE) % SIDE) * SIDE + (zz + SIDE) % SIDE}

    sibling = {"row": 1 - r}
    x_right, x_left = {"head": (x + 1) % heads}, {"head": (x + heads - 1) % heads}
    span_next, span_prior = {"ctx": (c + 1) % SIDE**2}, {"ctx": (c + SIDE**2 - 1) % SIDE**2}

    pos1, pos2 = jnp.where(r == 0, z, y), jnp.where(r == 0, y, z)

    def along1(d):
        there = (pos1 + d + SIDE) % SIDE
        return {"ctx": jnp.where(r == 0, y * SIDE + there, there * SIDE + z)}

    def along2(d):
        there = (pos2 + d + SIDE) % SIDE
        return {"ctx": jnp.where(r == 0, there * SIDE + z, y * SIDE + there)}

    def per_row(body):
        for rr in range(2):
            pl.when(r == rr)(functools.partial(body, rr))

    ids = {}

    def copy(name, src, dst, device):
        index = ids.setdefault(name, len(ids))
        return pltpu.make_async_remote_copy(
            src_ref=src,
            dst_ref=dst,
            send_sem=send.at[index],
            recv_sem=recv.at[index],
            device_id=device,
            device_id_type=pl.DeviceIdType.MESH,
        )

    class Weights:
        def __init__(self, name, bufs):
            self.name, self.bufs = name, bufs

        def slot(self, rr, away):
            i = (away + REACH + SIDE) % SIDE
            return self.bufs[rr].at[y, i] if rr == 0 else self.bufs[rr].at[i, z]

        def unit(self, rr, away, sub=None):
            i = (pos2 + away + SIDE) % SIDE
            if sub is None:
                return self.bufs[rr].at[i] if rr == 0 else self.bufs[rr].at[:, i]
            cut = pl.ds(sub * (2 * REACH + 1), (2 * REACH + 1, SIDE - 2 * REACH - 1)[sub])
            return self.bufs[rr].at[i, cut] if rr == 0 else self.bufs[rr].at[cut, i]

        def first(self, rr, move, arriving):
            d, away = move
            return copy(
                (self.name, "first", move),
                self.slot(rr, away - d if arriving else away),
                self.slot(rr, away - d),
                along1(d),
            )

        def first_begin(self, rr, moves):
            for move in moves:
                self.first(rr, move, False).start()

        def first_end(self, rr, moves):
            for move in reversed(moves):
                self.first(rr, move, True).wait_recv()

        def second(self, rr, move, arriving):
            d, away, sub = move
            ref = self.unit(rr, away - d if arriving else away, sub)
            return copy((self.name, "second", move), ref, ref, along2(d))

        def to_sibling(self, rr, away, sub=None):
            ref = self.unit(rr, away, sub)
            return copy((self.name, "sibling", away, sub), ref, ref, sibling)

        def pass_on(self, rr, move):
            d, away, sub = move
            self.to_sibling(rr, away - d, sub).start()

        def from_sibling(self, rr):
            self.to_sibling(1 - rr, 0).wait_recv()
            for d, away, sub in self.moves:
                self.to_sibling(1 - rr, away - d, sub).wait_recv()

        def finish(self, rr):
            for move in self.near + self.far:
                self.first(rr, move, False).wait_send()
            self.to_sibling(rr, 0).wait_send()
            for move in self.moves:
                self.second(rr, move, False).wait_send()
                self.to_sibling(rr, move[1] - move[0], move[2]).wait_send()

    kv, query = Weights("kv", (wkb, wvb)), Weights("q", (wq0, wq1))
    kv.near = [(2, 0), (-2, 0), (1, 0), (-1, 0)]
    kv.far = [(4, 0), (3, 0), (-3, 0)]
    query.near, query.far = [(2, 0), (-2, 0), (1, 0), (-1, 0)], [(2, -2), (1, -2), (-1, 2)]
    kv.one = [[(d, 0, sub) for d in (2, -2, 1, -1)] for sub in (0, 1)]
    kv.two = [
        [(1, -2, 0), (-1, 2, 0), (-2, 2, 0)],
        [(1, -2, 1), (-1, 2, 1), (2, -2, 1)],
    ]
    kv.moves = kv.one[0] + kv.one[1] + kv.two[0] + kv.two[1]

    def query_move(way, step, sub):
        return (way, -way * (step - 1), sub)

    query.steps = [(w, s, b) for s in (1, 2, 3) for b in (0, 1) for w in (1, -1)]
    query.steps += [(-1, SIDE // 2, 0), (1, SIDE // 2, 1)]
    query.moves = [query_move(*step) for step in query.steps]

    def query_begin(rr, sub):
        for way in (1, -1):
            query.second(rr, query_move(way, 1, sub), False).start()

    def query_step(rr, step, sub):
        for way in (1, -1):
            if (way, step, sub) in query.steps:
                query.second(rr, query_move(way, step, sub), True).wait_recv()
                if (way, step + 1, sub) in query.steps:
                    query.second(rr, query_move(way, step + 1, sub), False).start()
                query.pass_on(rr, query_move(way, step, sub))

    own_hidden = pltpu.make_async_copy(hid, hbuf.at[x], lsem.at[0])
    own_hidden.start()
    tables = pltpu.make_async_copy(moving_hbm, moving, lsem.at[3])
    tables.start()
    small = [
        pltpu.make_async_copy(src, dst, lsem.at[4 + i])
        for i, (src, dst) in enumerate(
            (
                (published_hbm, published),
                (vertical_hbm, vertical),
                (vcount_hbm, vcount),
                (slash_hbm, slash),
                (scount_hbm, scount),
            )
        )
    ]
    for one in small:
        one.start()

    def own_weights(rr):
        columns = pl.ds(0, left_cols) if rr == 0 else pl.ds(left_cols, wq.shape[1] - left_cols)
        return (
            pltpu.make_async_copy((wk, wv)[rr], kv.slot(rr, 0), lsem.at[1]),
            pltpu.make_async_copy(wq.at[:, columns], query.slot(rr, 0), lsem.at[2]),
        )

    per_row(lambda rr: [one.start() for one in own_weights(rr)] and None)

    barrier = pltpu.get_barrier_semaphore()
    partners = [along1(d) for d in FIRST_ORDER] + [along2(d) for d in (1, -1, 2, -2, 4)]
    partners += [sibling, x_right, x_left, span_next, span_prior]
    for device in partners:
        pl.semaphore_signal(barrier, inc=1, device_id=device, device_id_type=pl.DeviceIdType.MESH)
    pl.semaphore_wait(barrier, len(partners))

    def weights_begin(rr):
        first, second = own_weights(rr)
        first.wait()
        kv.first_begin(rr, kv.near + kv.far)
        second.wait()
        query.first_begin(rr, query.near)

    per_row(weights_begin)

    half = tokens // 2

    def feature(way, sub, far, arriving):
        away = way * ((2 if far else 1) if arriving else (1 if far else 0))
        ref = hbuf.at[(x - away + heads) % heads, pl.ds(sub * half, half)]
        return copy(("x", way, sub, far), ref, ref, x_right if way == 1 else x_left)

    own_hidden.wait()
    for way, sub in ((1, 0), (-1, 1), (1, 1), (-1, 0)):
        feature(way, sub, False, False).start()

    list_sends = [copy(("list", d), vertical_hbm.at[0], lists.at[i], along2(d)) for i, d in ((0, -1), (1, 1))]
    for one in list_sends:
        one.start()

    for one in small:
        one.wait()
    tables.wait()

    rows = lax.broadcasted_iota(jnp.int32, (tokens, tokens), 0)
    columns = lax.broadcasted_iota(jnp.int32, (tokens, tokens), 1)
    bias_local[...] = jnp.where(rows >= columns, 0.0, MASKED)
    back = rows - columns + tokens
    near = jnp.full((tokens, tokens), MASKED, F32)
    for e in range(slash.shape[-1]):
        offset = jnp.where((e < scount[0, 0]) & (c > 0), slash[0, 0, e], 0)
        near = jnp.where(back == offset, 0.0, near)
    bias_near[...] = near

    def kv_send(rr, moves):
        for move in moves:
            kv.second(rr, move, False).start()

    def kv_take(rr, moves):
        for move in moves:
            kv.second(rr, move, True).wait_recv()

    def kv_first(rr):
        kv.first_end(rr, kv.near)
        kv_send(rr, kv.one[0])
        kv.first_end(rr, kv.far)
        kv_send(rr, kv.one[1])
        query.first_end(rr, query.near)
        query.first_begin(rr, query.far)
        query_begin(rr, 0)
        kv.to_sibling(rr, 0).start()

    per_row(kv_first)
    for way, sub in ((1, 0), (-1, 1)):
        feature(way, sub, False, True).wait_recv()
        feature(way, sub, True, False).start()

    def spread(rr):
        for sub in (0, 1):
            kv_take(rr, kv.one[sub])
            kv_send(rr, kv.two[sub])
        for move in kv.one[0] + kv.one[1]:
            kv.pass_on(rr, move)
        query.first_end(rr, query.far)
        query_begin(rr, 1)
        query.to_sibling(rr, 0).start()
        query_step(rr, 1, 0)
        for sub in (0, 1):
            kv_take(rr, kv.two[sub])
            for move in kv.two[sub]:
                kv.pass_on(rr, move)
        query_step(rr, 1, 1)
        kv.from_sibling(rr)

    per_row(spread)
    for way, sub in ((1, 1), (-1, 0)):
        feature(way, sub, False, True).wait_recv()
    for way, sub in ((1, 0), (-1, 1)):
        feature(way, sub, True, True).wait_recv()

    def gathered(h, rr, one):
        def rank(i, pos):
            return (i - pos + REACH + SIDE) % SIDE

        down, across = [2 * h, 2 * h + 1], range(SIDE)
        if rr == 0:
            across = [rank(i, z) for i in across]
        else:
            down = [rank(i, y) for i in down]
        return jnp.concatenate([one[i, j] for i in down for j in across], axis=0)

    def project(h, *weights):
        block = jnp.concatenate([gathered(h, rr, one) for rr, one in weights], axis=1)
        return jnp.dot(hbuf[h], block, preferred_element_type=F32)

    def project_all(*weights):
        total = project(0, *weights)
        for h in range(1, heads):
            total = total + project(h, *weights)
        return total

    def query_steps(*steps):
        per_row(lambda rr: [query_step(rr, *one) for one in steps] and None)

    both = project_all((0, wkb), (1, wvb))
    keys = rotate(both[:, :width] + bk[...][None, :], moving[0], moving[1]).astype(BF16)
    kt[0] = keys.T
    vv[0] = (both[:, width:] + bv[...][None, :]).astype(BF16)

    here = pool.at[pos1, pos2 // 2]
    first_block = published[0, 0] == 0
    here[0] = jnp.where(first_block, kt[0, :, :BLOCK], kt[0, :, BLOCK:])
    here[1] = jnp.where(first_block, vv[0, :BLOCK], vv[0, BLOCK:])

    def alike(d, arriving):
        place = (pos2 - d + SIDE) % SIDE if arriving else pos2
        ref = pool.at[pos1, place // 2]
        return copy(("alike", d), ref, ref, along2(d))

    offsets = (0, 2, -2, 4)

    def around(way, step, o, arriving):
        i = (pos1 - way * (step if arriving else step - 1) + SIDE) % SIDE
        ref = pool.at[i, (pos2 + o + SIDE) % SIDE // 2]
        return copy(("round", way, step, o), ref, ref, along1(way))

    def ways(step, o):
        return (1, -1) if step < SIDE // 2 else (1,) if o in (0, 2) else (-1,)

    def round_begin(o):
        for way in (1, -1):
            around(way, 1, o, False).start()

    def round_step(step, o):
        for way in ways(step, o):
            around(way, step, o, True).wait_recv()
            if step < SIDE // 2 and way in ways(step + 1, o):
                around(way, step + 1, o, False).start()

    for d in (2, -2, 4):
        alike(d, False).start()
    round_begin(0)
    query_steps((2, 0), (2, 1))
    round_step(1, 0)
    for d in (2, -2):
        alike(d, True).wait_recv()
        round_begin(-d)
    for way, sub in ((1, 0), (-1, 1), (1, 1), (-1, 0)):
        feature(way, sub, False, False).wait_send()
    for way, sub in ((1, 0), (-1, 1)):
        feature(way, sub, True, False).wait_send()
    per_row(kv.finish)
    query_steps((3, 0))
    alike(4, True).wait_recv()
    round_begin(4)
    round_step(2, 0)
    round_step(1, 2)
    round_step(1, -2)
    query_steps((3, 1))
    round_step(1, 4)
    round_step(3, 0)
    round_step(2, 2)
    round_step(2, -2)
    query_steps((4, 0), (4, 1))
    round_step(2, 4)
    round_step(4, 0)
    round_step(3, 2)
    round_step(3, -2)
    behind = [
        copy(("prior", "k"), kt.at[0], kt.at[1], span_next),
        copy(("prior", "v"), vv.at[0], vv.at[1], span_next),
    ]
    for one in behind:
        one.start()
    per_row(query.from_sibling)

    qraw[:, :left_cols] = project_all((0, wq0))
    round_step(3, 4)
    qraw[:, left_cols:] = project_all((1, wq1))

    def rotate_head(g):
        columns = pl.ds(pl.multiple_of(g * width, width), width)
        raw = qraw[:, columns] + bq[columns][None, :]
        swapped = pltpu.roll(raw, width // 2, axis=1)
        ql[g] = (raw * moving[0] + swapped * moving[1]).astype(BF16)
        qn[g] = (raw * moving[2] + swapped * moving[3]).astype(BF16)
        qf[g] = (raw * fixed[0:1] + swapped * fixed[1:2]).astype(BF16)

    pl.loop(0, 4)(rotate_head)
    round_step(4, 2)
    round_step(4, -2)
    pl.loop(4, group)(rotate_head)
    for one in behind:
        one.wait_recv()

    def close_part(g):
        local = jnp.dot(ql[g], kt[0], preferred_element_type=F32) * score_scale + bias_local[...]
        slashed = jnp.dot(qn[g], kt[1], preferred_element_type=F32) * score_scale + bias_near[...]
        highest = jnp.maximum(
            jnp.max(local, axis=1, keepdims=True), jnp.max(slashed, axis=1, keepdims=True)
        )
        local, slashed = jnp.exp2(local - highest), jnp.exp2(slashed - highest)
        total = jnp.sum(local, axis=1, keepdims=True) + jnp.sum(slashed, axis=1, keepdims=True)
        top1[g] = jnp.broadcast_to(highest, (tokens, width))
        sum1[g] = jnp.broadcast_to(total, (tokens, width))
        acc1[g] = jnp.dot(local.astype(BF16), vv[0], preferred_element_type=F32) + jnp.dot(
            slashed.astype(BF16), vv[1], preferred_element_type=F32
        )

    pl.loop(0, 1)(close_part)
    round_step(4, 4)

    def place_of(span):
        across, down = span % SIDE, span // SIDE
        return jnp.where(r == 0, across, down), jnp.where(r == 0, down, across)

    for one in list_sends:
        one.wait_recv()
    each = slots // 2
    trades = {}
    for which in range(2):
        for side, d in ((0, 1), (1, -1)):
            for e in range(each):
                one, two = place_of(lists[side, 0, side * each + e])
                chosen[side, which, e] = pool[one, two // 2, which]
            src, dst = chosen.at[side, which], got.at[side, which]
            trades[side, which] = copy(("trade", d, which), src, dst, along2(d))
            trades[side, which].start()
    pl.loop(1, group)(close_part)

    def listed(e, which):
        one, two = place_of(vertical[0, 0, e])
        traded = got[e // each, which, e % each]
        return jnp.where(two % 2 == pos2 % 2, pool[one, two // 2, which], traded)

    per_row(query.finish)
    for d in (4, 2, -2):
        alike(d, False).wait_send()
    for o in offsets:
        for step in (1, 2, 3, 4):
            for way in ways(step, o):
                around(way, step, o, False).wait_send()
    for one in behind + list_sends:
        one.wait_send()
    for side in range(2):
        trades[side, 0].wait_recv()
    for e in range(slots):
        kft[:, e * BLOCK : (e + 1) * BLOCK] = listed(e, 0)
    place = lax.broadcasted_iota(jnp.int32, (1, slots * BLOCK), 1)
    bias_far = jnp.where(place < vcount[0, 0] * BLOCK, 0.0, MASKED)

    def far_scores(g):
        return jnp.dot(qf[g], kft[...], preferred_element_type=F32) * score_scale + bias_far

    def far_part(g, scores):
        before = top1[g][:, :1]
        highest = jnp.maximum(before, jnp.max(scores, axis=1, keepdims=True))
        weights = jnp.exp2(scores - highest)
        fade = jnp.exp2(before - highest)
        total = sum1[g][:, :1] * fade + jnp.sum(weights, axis=1, keepdims=True)
        combined = acc1[g] * fade + jnp.dot(
            weights.astype(BF16), vft[...], preferred_element_type=F32
        )
        columns = pl.ds(g * width, width)
        out[:, columns] = (combined / total).astype(BF16)

    scores = far_scores(0)
    for side in range(2):
        trades[side, 1].wait_recv()
    for e in range(slots):
        vft[e * BLOCK : (e + 1) * BLOCK] = listed(e, 1)
    for g in range(group):
        far_part(g, scores)
        if g + 1 < group:
            scores = far_scores(g + 1)

    for one in trades.values():
        one.wait_send()


def on_device(
    hidden_states, w_query, key_weight_matrix, value_weight_matrix, bias_query, bias_key,
    value_bias_vector, published, vertical, vcount, slash_offsets, scount,
):
    tokens, part = hidden_states.shape
    depth, width = key_weight_matrix.shape
    columns = w_query.shape[1]
    group = columns // width
    heads = lax.axis_size("head")
    slots = vertical.shape[-1]
    left = (group // 2) * width
    moving, fixed = rope_tables(tokens, width)
    hbm = pl.BlockSpec(memory_space=pl.ANY)
    vmem = pl.BlockSpec(memory_space=pltpu.VMEM)
    copies = 160
    return pl.pallas_call(
        kernel,
        out_shape=pltpu.VMEM((tokens, columns), BF16),
        in_specs=[hbm] * 10 + [vmem] * 4,
        out_specs=pl.BlockSpec(memory_space=pltpu.VMEM),
        scratch_shapes=[
            pltpu.VMEM(moving.shape, F32),
            pltpu.SMEM(published.shape, jnp.int32),
            pltpu.SMEM(vertical.shape, jnp.int32),
            pltpu.SMEM(vcount.shape, jnp.int32),
            pltpu.SMEM(slash_offsets.shape, jnp.int32),
            pltpu.SMEM(scount.shape, jnp.int32),
            pltpu.VMEM((heads, tokens, part), BF16),
            pltpu.VMEM((SIDE, SIDE, depth, width), BF16),
            pltpu.VMEM((SIDE, SIDE, depth, width), BF16),
            pltpu.VMEM((SIDE, SIDE, depth, left), BF16),
            pltpu.VMEM((SIDE, SIDE, depth, columns - left), BF16),
            pltpu.VMEM((SIDE, SIDE // 2, 2, BLOCK, width), BF16),
            pltpu.VMEM((2, 2, slots // 2, BLOCK, width), BF16),
            pltpu.VMEM((2, 2, slots // 2, BLOCK, width), BF16),
            pltpu.SMEM((2, 1, slots), jnp.int32),
            pltpu.VMEM((2, width, tokens), BF16),
            pltpu.VMEM((2, tokens, width), BF16),
            pltpu.VMEM((tokens, columns), F32),
            pltpu.VMEM((group, tokens, width), BF16),
            pltpu.VMEM((group, tokens, width), BF16),
            pltpu.VMEM((group, tokens, width), BF16),
            pltpu.VMEM((width, slots * BLOCK), BF16),
            pltpu.VMEM((slots * BLOCK, width), BF16),
            pltpu.VMEM((group, tokens, width), F32),
            pltpu.VMEM((group, tokens, width), F32),
            pltpu.VMEM((group, tokens, width), F32),
            pltpu.VMEM((tokens, tokens), F32),
            pltpu.VMEM((tokens, tokens), F32),
            pltpu.SemaphoreType.DMA((copies,)),
            pltpu.SemaphoreType.DMA((copies,)),
            pltpu.SemaphoreType.DMA((9,)),
            pltpu.SemaphoreType.DMA((group,)),
        ],
        compiler_params=pltpu.CompilerParams(
            collective_id=0, has_side_effects=True, vmem_limit_bytes=56 * 1024 * 1024
        ),
        cost_estimate=pl.CostEstimate(
            flops=4 * 10**9, bytes_accessed=10**7, transcendentals=3 * 10**6
        ),
    )(
        hidden_states, key_weight_matrix, value_weight_matrix, w_query, jnp.asarray(moving),
        published, vertical, vcount, slash_offsets, scount,
        bias_query, bias_key, value_bias_vector, jnp.asarray(fixed),
    )


def solution(mesh):
    spans, kept = P(("row", "ctx"), "head"), P(("row", "ctx"), "head", None)
    weight, bias = P("ctx", "head"), P("head")
    return jax.shard_map(
        on_device,
        mesh=mesh,
        in_specs=(spans, weight, weight, weight, bias, bias, bias, spans, kept, spans, kept, spans),
        out_specs=spans,
        check_vma=False,
    )
```

```python
import functools

import jax
import jax.numpy as jnp
import numpy as np
from jax import lax
from jax.experimental import pallas as pl
from jax.experimental.pallas import tpu as pltpu
from jax.sharding import PartitionSpec as P

BLOCK = 128
SIDE = 8
MASKED = -1e30
FIRST_ORDER = (4, 3, -3, 2, -2, 1, -1)
REACH = 2
LOG2E = 1.4426950408889634
BF16, F32 = jnp.bfloat16, jnp.float32


def rope_tables(tokens, width):
    exponents = np.arange(0, width, 2).astype(np.float32) / np.float32(width)
    inverse = np.power(np.float32(10000000.0), -exponents).astype(np.float32)
    places = np.arange(tokens).astype(np.float32)

    def pair(positions):
        angles = (positions[:, None] * inverse[None, :]).astype(np.float32).astype(np.float64)
        cosine, sine = np.cos(angles), np.sin(angles)
        return [
            np.concatenate([cosine, cosine], axis=1).astype(np.float32),
            np.concatenate([-sine, sine], axis=1).astype(np.float32),
        ]

    moving = np.stack(pair(places) + pair(places + np.float32(tokens)))
    fixed = np.concatenate(pair(np.full((1,), 2 * tokens - 1, np.float32)))
    return moving, fixed


def rotate(rows, cosine, sine):
    return rows * cosine + pltpu.roll(rows, rows.shape[-1] // 2, axis=1) * sine


def kernel(
    hid, wk, wv, wq, moving_hbm, published_hbm, vertical_hbm, vcount_hbm, slash_hbm, scount_hbm,
    bq_hbm, bk_hbm, bv_hbm, fixed_hbm,
    out,
    bq, bk, bv, fixed, moving, published, vertical, vcount, slash, scount, hbuf, wkb, wvb, wq0, wq1, pool, chosen, got, lists, kt, vv, qraw, ql, qn, qf, kft, vft,
    top1, sum1, acc1, bias_local, bias_near,
    send, recv, lsem, osem,
):
    tokens, part = hid.shape
    width = wk.shape[1]
    group = wq.shape[1] // width
    left_cols = wq0.shape[-1]
    heads = hbuf.shape[0]
    slots = vertical.shape[-1]
    x, c, r = lax.axis_index("head"), lax.axis_index("ctx"), lax.axis_index("row")
    y, z = c // SIDE, c % SIDE
    score_scale = width**-0.5 * LOG2E

    def at(yy, zz):
        return {"ctx": ((yy + SIDE) % SIDE) * SIDE + (zz + SIDE) % SIDE}

    sibling = {"row": 1 - r}
    x_right, x_left = {"head": (x + 1) % heads}, {"head": (x + heads - 1) % heads}
    span_next, span_prior = {"ctx": (c + 1) % SIDE**2}, {"ctx": (c + SIDE**2 - 1) % SIDE**2}

    pos1, pos2 = jnp.where(r == 0, z, y), jnp.where(r == 0, y, z)

    def along1(d):
        there = (pos1 + d + SIDE) % SIDE
        return {"ctx": jnp.where(r == 0, y * SIDE + there, there * SIDE + z)}

    def along2(d):
        there = (pos2 + d + SIDE) % SIDE
        return {"ctx": jnp.where(r == 0, there * SIDE + z, y * SIDE + there)}

    def per_row(body):
        for rr in range(2):
            pl.when(r == rr)(functools.partial(body, rr))

    ids = {}

    def copy(name, src, dst, device):
        index = ids.setdefault(name, len(ids))
        return pltpu.make_async_remote_copy(
            src_ref=src,
            dst_ref=dst,
            send_sem=send.at[index],
            recv_sem=recv.at[index],
            device_id=device,
            device_id_type=pl.DeviceIdType.MESH,
        )

    class Weights:
        def __init__(self, name, bufs):
            self.name, self.bufs = name, bufs

        def slot(self, rr, away):
            i = (away + REACH + SIDE) % SIDE
            return self.bufs[rr].at[y, i] if rr == 0 else self.bufs[rr].at[i, z]

        def unit(self, rr, away, sub=None):
            i = (pos2 + away + SIDE) % SIDE
            if sub is None:
                return self.bufs[rr].at[i] if rr == 0 else self.bufs[rr].at[:, i]
            cut = pl.ds(sub * (2 * REACH + 1), (2 * REACH + 1, SIDE - 2 * REACH - 1)[sub])
            return self.bufs[rr].at[i, cut] if rr == 0 else self.bufs[rr].at[cut, i]

        def first(self, rr, move, arriving):
            d, away = move
            return copy(
                (self.name, "first", move),
                self.slot(rr, away - d if arriving else away),
                self.slot(rr, away - d),
                along1(d),
            )

        def first_begin(self, rr, moves):
            for move in moves:
                self.first(rr, move, False).start()

        def first_end(self, rr, moves):
            for move in reversed(moves):
                self.first(rr, move, True).wait_recv()

        def second(self, rr, move, arriving):
            d, away, sub = move
            ref = self.unit(rr, away - d if arriving else away, sub)
            return copy((self.name, "second", move), ref, ref, along2(d))

        def to_sibling(self, rr, away, sub=None):
            ref = self.unit(rr, away, sub)
            return copy((self.name, "sibling", away, sub), ref, ref, sibling)

        def pass_on(self, rr, move):
            d, away, sub = move
            self.to_sibling(rr, away - d, sub).start()

        def from_sibling(self, rr):
            self.to_sibling(1 - rr, 0).wait_recv()
            for d, away, sub in self.moves:
                self.to_sibling(1 - rr, away - d, sub).wait_recv()

        def finish(self, rr):
            for move in self.near + self.far:
                self.first(rr, move, False).wait_send()
            self.to_sibling(rr, 0).wait_send()
            for move in self.moves:
                self.second(rr, move, False).wait_send()
                self.to_sibling(rr, move[1] - move[0], move[2]).wait_send()

    kv, query = Weights("kv", (wkb, wvb)), Weights("q", (wq0, wq1))
    kv.near = [(2, 0), (-2, 0), (1, 0), (-1, 0)]
    kv.far = [(4, 0), (3, 0), (-3, 0)]
    query.near, query.far = [(2, 0), (-2, 0), (1, 0), (-1, 0)], [(2, -2), (1, -2), (-1, 2)]
    kv.one = [[(d, 0, sub) for d in (2, -2, 1, -1)] for sub in (0, 1)]
    kv.two = [
        [(1, -2, 0), (-1, 2, 0), (-2, 2, 0)],
        [(1, -2, 1), (-1, 2, 1), (2, -2, 1)],
    ]
    kv.moves = kv.one[0] + kv.one[1] + kv.two[0] + kv.two[1]

    def query_move(way, step, sub):
        return (way, -way * (step - 1), sub)

    query.steps = [(w, s, b) for s in (1, 2, 3) for b in (0, 1) for w in (1, -1)]
    query.steps += [(-1, SIDE // 2, 0), (1, SIDE // 2, 1)]
    query.moves = [query_move(*step) for step in query.steps]

    def query_begin(rr, sub):
        for way in (1, -1):
            query.second(rr, query_move(way, 1, sub), False).start()

    def query_step(rr, step, sub):
        for way in (1, -1):
            if (way, step, sub) in query.steps:
                query.second(rr, query_move(way, step, sub), True).wait_recv()
                if (way, step + 1, sub) in query.steps:
                    query.second(rr, query_move(way, step + 1, sub), False).start()
                query.pass_on(rr, query_move(way, step, sub))

    barrier = pltpu.get_barrier_semaphore()
    partners = [along1(d) for d in FIRST_ORDER] + [along2(d) for d in (1, -1, 2, -2, 4)]
    partners += [sibling, x_right, x_left, span_next, span_prior]
    for device in partners:
        pl.semaphore_signal(barrier, inc=1, device_id=device, device_id_type=pl.DeviceIdType.MESH)

    own_hidden = pltpu.make_async_copy(hid, hbuf.at[x], lsem.at[0])
    own_hidden.start()
    tables = pltpu.make_async_copy(moving_hbm, moving, lsem.at[3])
    tables.start()
    small = [
        pltpu.make_async_copy(src, dst, lsem.at[4 + i])
        for i, (src, dst) in enumerate(
            (
                (published_hbm, published),
                (vertical_hbm, vertical),
                (vcount_hbm, vcount),
                (slash_hbm, slash),
                (scount_hbm, scount),
                (bq_hbm, bq),
                (bk_hbm, bk),
                (bv_hbm, bv),
                (fixed_hbm, fixed),
            )
        )
    ]
    for one in small:
        one.start()

    def own_weights(rr):
        columns = pl.ds(0, left_cols) if rr == 0 else pl.ds(left_cols, wq.shape[1] - left_cols)
        return (
            pltpu.make_async_copy((wk, wv)[rr], kv.slot(rr, 0), lsem.at[1]),
            pltpu.make_async_copy(wq.at[:, columns], query.slot(rr, 0), lsem.at[2]),
        )

    per_row(lambda rr: [one.start() for one in own_weights(rr)] and None)

    pl.semaphore_wait(barrier, len(partners))

    def weights_begin(rr):
        first, second = own_weights(rr)
        first.wait()
        kv.first_begin(rr, kv.near + kv.far)
        second.wait()
        query.first_begin(rr, query.near)

    per_row(weights_begin)

    half = tokens // 2

    def feature(way, sub, far, arriving):
        away = way * ((2 if far else 1) if arriving else (1 if far else 0))
        ref = hbuf.at[(x - away + heads) % heads, pl.ds(sub * half, half)]
        return copy(("x", way, sub, far), ref, ref, x_right if way == 1 else x_left)

    own_hidden.wait()
    for way, sub in ((1, 0), (-1, 1), (1, 1), (-1, 0)):
        feature(way, sub, False, False).start()

    list_sends = [copy(("list", d), vertical_hbm.at[0], lists.at[i], along2(d)) for i, d in ((0, -1), (1, 1))]
    for one in list_sends:
        one.start()

    for one in small:
        one.wait()
    tables.wait()

    rows = lax.broadcasted_iota(jnp.int32, (tokens, tokens), 0)
    columns = lax.broadcasted_iota(jnp.int32, (tokens, tokens), 1)
    bias_local[...] = jnp.where(rows >= columns, 0.0, MASKED)
    back = rows - columns + tokens
    near = jnp.full((tokens, tokens), MASKED, F32)
    for e in range(slash.shape[-1]):
        offset = jnp.where((e < scount[0, 0]) & (c > 0), slash[0, 0, e], 0)
        near = jnp.where(back == offset, 0.0, near)
    bias_near[...] = near

    def kv_send(rr, moves):
        for move in moves:
            kv.second(rr, move, False).start()

    def kv_take(rr, moves):
        for move in moves:
            kv.second(rr, move, True).wait_recv()

    def kv_first(rr):
        kv.first_end(rr, kv.near)
        kv_send(rr, kv.one[0])
        kv.first_end(rr, kv.far)
        kv_send(rr, kv.one[1])
        query.first_end(rr, query.near)
        query.first_begin(rr, query.far)
        query_begin(rr, 0)
        kv.to_sibling(rr, 0).start()

    per_row(kv_first)
    for way, sub in ((1, 0), (-1, 1)):
        feature(way, sub, False, True).wait_recv()
        feature(way, sub, True, False).start()

    def spread(rr):
        for sub in (0, 1):
            kv_take(rr, kv.one[sub])
            kv_send(rr, kv.two[sub])
        for move in kv.one[0] + kv.one[1]:
            kv.pass_on(rr, move)
        query.first_end(rr, query.far)
        query_begin(rr, 1)
        query.to_sibling(rr, 0).start()
        query_step(rr, 1, 0)
        for sub in (0, 1):
            kv_take(rr, kv.two[sub])
            for move in kv.two[sub]:
                kv.pass_on(rr, move)
        query_step(rr, 1, 1)
        kv.from_sibling(rr)

    per_row(spread)
    for way, sub in ((1, 1), (-1, 0)):
        feature(way, sub, False, True).wait_recv()
    for way, sub in ((1, 0), (-1, 1)):
        feature(way, sub, True, True).wait_recv()

    def gathered(h, rr, one):
        def rank(i, pos):
            return (i - pos + REACH + SIDE) % SIDE

        down, across = [2 * h, 2 * h + 1], range(SIDE)
        if rr == 0:
            across = [rank(i, z) for i in across]
        else:
            down = [rank(i, y) for i in down]
        return jnp.concatenate([one[i, j] for i in down for j in across], axis=0)

    def project(h, *weights):
        block = jnp.concatenate([gathered(h, rr, one) for rr, one in weights], axis=1)
        return jnp.dot(hbuf[h], block, preferred_element_type=F32)

    def project_all(*weights):
        total = project(0, *weights)
        for h in range(1, heads):
            total = total + project(h, *weights)
        return total

    def query_steps(*steps):
        per_row(lambda rr: [query_step(rr, *one) for one in steps] and None)

    both = project_all((0, wkb), (1, wvb))
    keys = rotate(both[:, :width] + bk[...][None, :], moving[0], moving[1]).astype(BF16)
    kt[0] = keys.T
    vv[0] = (both[:, width:] + bv[...][None, :]).astype(BF16)

    here = pool.at[pos1, pos2 // 2]
    first_block = published[0, 0] == 0
    here[0] = jnp.where(first_block, kt[0, :, :BLOCK], kt[0, :, BLOCK:])
    here[1] = jnp.where(first_block, vv[0, :BLOCK], vv[0, BLOCK:])

    def alike(d, arriving):
        place = (pos2 - d + SIDE) % SIDE if arriving else pos2
        ref = pool.at[pos1, place // 2]
        return copy(("alike", d), ref, ref, along2(d))

    offsets = (0, 2, -2, 4)

    def around(way, step, o, arriving):
        i = (pos1 - way * (step if arriving else step - 1) + SIDE) % SIDE
        ref = pool.at[i, (pos2 + o + SIDE) % SIDE // 2]
        return copy(("round", way, step, o), ref, ref, along1(way))

    def ways(step, o):
        return (1, -1) if step < SIDE // 2 else (-1,)

    def round_begin(o):
        for way in (1, -1):
            around(way, 1, o, False).start()

    def round_step(step, o):
        for way in ways(step, o):
            around(way, step, o, True).wait_recv()
            if step < SIDE // 2 and way in ways(step + 1, o):
                around(way, step + 1, o, False).start()

    for d in (2, -2, 4):
        alike(d, False).start()
    round_begin(0)
    query_steps((2, 0), (2, 1))
    round_step(1, 0)
    for d in (2, -2):
        alike(d, True).wait_recv()
        round_begin(-d)
    for way, sub in ((1, 0), (-1, 1), (1, 1), (-1, 0)):
        feature(way, sub, False, False).wait_send()
    for way, sub in ((1, 0), (-1, 1)):
        feature(way, sub, True, False).wait_send()
    per_row(kv.finish)
    alike(4, True).wait_recv()
    round_begin(4)
    round_step(2, 0)
    round_step(1, 2)
    round_step(1, -2)
    query_steps((3, 0))
    round_step(1, 4)
    query_steps((3, 1))
    behind = [
        copy(("prior", "k"), kt.at[0], kt.at[1], span_next),
        copy(("prior", "v"), vv.at[0], vv.at[1], span_next),
    ]
    for one in behind:
        one.start()
    round_step(3, 0)
    round_step(2, 2)
    round_step(2, -2)

    def last_steps(rr):
        for sub in (0, 1):
            query_step(rr, SIDE // 2, sub)

    per_row(lambda rr: query.from_sibling(rr) if rr else last_steps(rr))

    def rotate_head(g):
        columns = pl.ds(pl.multiple_of(g * width, width), width)
        raw = qraw[:, columns] + bq[columns][None, :]
        swapped = pltpu.roll(raw, width // 2, axis=1)
        ql[g] = (raw * moving[0] + swapped * moving[1]).astype(BF16)
        qn[g] = (raw * moving[2] + swapped * moving[3]).astype(BF16)
        qf[g] = (raw * fixed[0:1] + swapped * fixed[1:2]).astype(BF16)

    left_heads = left_cols // width
    qraw[:, :left_cols] = project_all((0, wq0))
    round_step(2, 4)
    round_step(4, 0)
    round_step(3, 2)
    round_step(3, -2)
    pl.loop(0, left_heads)(rotate_head)
    per_row(lambda rr: last_steps(rr) if rr else query.from_sibling(rr))
    round_step(3, 4)
    qraw[:, left_cols:] = project_all((1, wq1))
    round_step(4, 2)
    round_step(4, -2)
    pl.loop(left_heads, group)(rotate_head)
    for one in behind:
        one.wait_recv()

    def close_part(g):
        local = jnp.dot(ql[g], kt[0], preferred_element_type=F32) * score_scale + bias_local[...]
        slashed = jnp.dot(qn[g], kt[1], preferred_element_type=F32) * score_scale + bias_near[...]
        highest = jnp.maximum(
            jnp.max(local, axis=1, keepdims=True), jnp.max(slashed, axis=1, keepdims=True)
        )
        local, slashed = jnp.exp2(local - highest), jnp.exp2(slashed - highest)
        total = jnp.sum(local, axis=1, keepdims=True) + jnp.sum(slashed, axis=1, keepdims=True)
        top1[g] = jnp.broadcast_to(highest, (tokens, width))
        sum1[g] = jnp.broadcast_to(total, (tokens, width))
        acc1[g] = jnp.dot(local.astype(BF16), vv[0], preferred_element_type=F32) + jnp.dot(
            slashed.astype(BF16), vv[1], preferred_element_type=F32
        )

    pl.loop(0, 1)(close_part)
    round_step(4, 4)

    def place_of(span):
        across, down = span % SIDE, span // SIDE
        return jnp.where(r == 0, across, down), jnp.where(r == 0, down, across)

    for one in list_sends:
        one.wait_recv()
    each = slots // 2
    trades = {}
    for which in range(2):
        for side, d in ((0, 1), (1, -1)):
            for e in range(each):
                one, two = place_of(lists[side, 0, side * each + e])
                chosen[side, which, e] = pool[one, two // 2, which]
            src, dst = chosen.at[side, which], got.at[side, which]
            trades[side, which] = copy(("trade", d, which), src, dst, along2(d))
            trades[side, which].start()
    pl.loop(1, group)(close_part)

    def listed(e, which):
        one, two = place_of(vertical[0, 0, e])
        traded = got[e // each, which, e % each]
        return jnp.where(two % 2 == pos2 % 2, pool[one, two // 2, which], traded)

    per_row(query.finish)
    for d in (4, 2, -2):
        alike(d, False).wait_send()
    for o in offsets:
        for step in (1, 2, 3, 4):
            for way in ways(step, o):
                around(way, step, o, False).wait_send()
    for one in behind + list_sends:
        one.wait_send()
    for side in range(2):
        trades[side, 0].wait_recv()
    for e in range(slots):
        kft[:, e * BLOCK : (e + 1) * BLOCK] = listed(e, 0)
    place = lax.broadcasted_iota(jnp.int32, (1, slots * BLOCK), 1)
    bias_far = jnp.where(place < vcount[0, 0] * BLOCK, 0.0, MASKED)

    def far_scores(g):
        return jnp.dot(qf[g], kft[...], preferred_element_type=F32) * score_scale + bias_far

    def far_part(g, scores):
        before = top1[g][:, :1]
        highest = jnp.maximum(before, jnp.max(scores, axis=1, keepdims=True))
        weights = jnp.exp2(scores - highest)
        fade = jnp.exp2(before - highest)
        total = sum1[g][:, :1] * fade + jnp.sum(weights, axis=1, keepdims=True)
        combined = acc1[g] * fade + jnp.dot(
            weights.astype(BF16), vft[...], preferred_element_type=F32
        )
        columns = pl.ds(g * width, width)
        out[:, columns] = (combined / total).astype(BF16)

    scores = far_scores(0)
    for side in range(2):
        trades[side, 1].wait_recv()
    for e in range(slots):
        vft[e * BLOCK : (e + 1) * BLOCK] = listed(e, 1)
    for g in range(group):
        following = far_scores(g + 1) if g + 1 < group else None
        far_part(g, scores)
        scores = following

    for one in trades.values():
        one.wait_send()


def on_device(
    hidden_states, w_query, key_weight_matrix, value_weight_matrix, bias_query, bias_key,
    value_bias_vector, published, vertical, vcount, slash_offsets, scount,
):
    tokens, part = hidden_states.shape
    depth, width = key_weight_matrix.shape
    columns = w_query.shape[1]
    group = columns // width
    heads = lax.axis_size("head")
    slots = vertical.shape[-1]
    left = (group // 2) * width
    moving, fixed = rope_tables(tokens, width)
    hbm = pl.BlockSpec(memory_space=pl.ANY)
    copies = 160
    return pl.pallas_call(
        kernel,
        out_shape=pltpu.VMEM((tokens, columns), BF16),
        in_specs=[hbm] * 14,
        out_specs=pl.BlockSpec(memory_space=pltpu.VMEM),
        scratch_shapes=[
            pltpu.VMEM(bias_query.shape, F32),
            pltpu.VMEM(bias_key.shape, F32),
            pltpu.VMEM(value_bias_vector.shape, F32),
            pltpu.VMEM(fixed.shape, F32),
            pltpu.VMEM(moving.shape, F32),
            pltpu.SMEM(published.shape, jnp.int32),
            pltpu.SMEM(vertical.shape, jnp.int32),
            pltpu.SMEM(vcount.shape, jnp.int32),
            pltpu.SMEM(slash_offsets.shape, jnp.int32),
            pltpu.SMEM(scount.shape, jnp.int32),
            pltpu.VMEM((heads, tokens, part), BF16),
            pltpu.VMEM((SIDE, SIDE, depth, width), BF16),
            pltpu.VMEM((SIDE, SIDE, depth, width), BF16),
            pltpu.VMEM((SIDE, SIDE, depth, left), BF16),
            pltpu.VMEM((SIDE, SIDE, depth, columns - left), BF16),
            pltpu.VMEM((SIDE, SIDE // 2, 2, BLOCK, width), BF16),
            pltpu.VMEM((2, 2, slots // 2, BLOCK, width), BF16),
            pltpu.VMEM((2, 2, slots // 2, BLOCK, width), BF16),
            pltpu.SMEM((2, 1, slots), jnp.int32),
            pltpu.VMEM((2, width, tokens), BF16),
            pltpu.VMEM((2, tokens, width), BF16),
            pltpu.VMEM((tokens, columns), F32),
            pltpu.VMEM((group, tokens, width), BF16),
            pltpu.VMEM((group, tokens, width), BF16),
            pltpu.VMEM((group, tokens, width), BF16),
            pltpu.VMEM((width, slots * BLOCK), BF16),
            pltpu.VMEM((slots * BLOCK, width), BF16),
            pltpu.VMEM((group, tokens, width), F32),
            pltpu.VMEM((group, tokens, width), F32),
            pltpu.VMEM((group, tokens, width), F32),
            pltpu.VMEM((tokens, tokens), F32),
            pltpu.VMEM((tokens, tokens), F32),
            pltpu.SemaphoreType.DMA((copies,)),
            pltpu.SemaphoreType.DMA((copies,)),
            pltpu.SemaphoreType.DMA((13,)),
            pltpu.SemaphoreType.DMA((group,)),
        ],
        compiler_params=pltpu.CompilerParams(
            collective_id=0, has_side_effects=True, vmem_limit_bytes=56 * 1024 * 1024
        ),
        cost_estimate=pl.CostEstimate(
            flops=4 * 10**9, bytes_accessed=10**7, transcendentals=3 * 10**6
        ),
    )(
        hidden_states, key_weight_matrix, value_weight_matrix, w_query, jnp.asarray(moving),
        published, vertical, vcount, slash_offsets, scount,
        bias_query, bias_key, value_bias_vector, jnp.asarray(fixed),
    )


def solution(mesh):
    spans, kept = P(("row", "ctx"), "head"), P(("row", "ctx"), "head", None)
    weight, bias = P("ctx", "head"), P("head")
    return jax.shard_map(
        on_device,
        mesh=mesh,
        in_specs=(spans, weight, weight, weight, bias, bias, bias, spans, kept, spans, kept, spans),
        out_specs=spans,
        check_vma=False,
    )
```

```python
import functools

import jax
import jax.numpy as jnp
import numpy as np
from jax import lax
from jax.experimental import pallas as pl
from jax.experimental.pallas import tpu as pltpu
from jax.sharding import PartitionSpec as P

BLOCK = 128
SIDE = 8
MASKED = -1e30
FIRST_ORDER = (4, 3, -3, 2, -2, 1, -1)
REACH = 2
LOG2E = 1.4426950408889634
BF16, F32 = jnp.bfloat16, jnp.float32


def rope_tables(tokens, width):
    exponents = np.arange(0, width, 2).astype(np.float32) / np.float32(width)
    inverse = np.power(np.float32(10000000.0), -exponents).astype(np.float32)
    places = np.arange(tokens).astype(np.float32)

    def pair(positions):
        angles = (positions[:, None] * inverse[None, :]).astype(np.float32).astype(np.float64)
        cosine, sine = np.cos(angles), np.sin(angles)
        return [
            np.concatenate([cosine, cosine], axis=1).astype(np.float32),
            np.concatenate([-sine, sine], axis=1).astype(np.float32),
        ]

    moving = np.stack(pair(places) + pair(places + np.float32(tokens)))
    fixed = np.concatenate(pair(np.full((1,), 2 * tokens - 1, np.float32)))
    return moving, fixed


def rotate(rows, cosine, sine):
    return rows * cosine + pltpu.roll(rows, rows.shape[-1] // 2, axis=1) * sine


def kernel(
    hid, wk, wv, wq, moving_hbm, published_hbm, vertical_hbm, vcount_hbm, slash_hbm, scount_hbm,
    bq_hbm, bk_hbm, bv_hbm, fixed_hbm,
    out,
    bq, bk, bv, fixed, moving, published, vertical, vcount, slash, scount, hbuf, wkb, wvb, wq0, wq1, pool, chosen, got, lists, kt, vv, qraw, ql, qn, qf, kft, vft,
    top1, sum1, acc1, bias_local, bias_near,
    send, recv, lsem, osem,
):
    tokens, part = hid.shape
    width = wk.shape[1]
    group = wq.shape[1] // width
    left_cols = wq0.shape[-1]
    heads = hbuf.shape[0]
    slots = vertical.shape[-1]
    x, c, r = lax.axis_index("head"), lax.axis_index("ctx"), lax.axis_index("row")
    y, z = c // SIDE, c % SIDE
    score_scale = width**-0.5 * LOG2E

    def at(yy, zz):
        return {"ctx": ((yy + SIDE) % SIDE) * SIDE + (zz + SIDE) % SIDE}

    sibling = {"row": 1 - r}
    x_right, x_left = {"head": (x + 1) % heads}, {"head": (x + heads - 1) % heads}
    span_next, span_prior = {"ctx": (c + 1) % SIDE**2}, {"ctx": (c + SIDE**2 - 1) % SIDE**2}

    pos1, pos2 = jnp.where(r == 0, z, y), jnp.where(r == 0, y, z)

    def along1(d):
        there = (pos1 + d + SIDE) % SIDE
        return {"ctx": jnp.where(r == 0, y * SIDE + there, there * SIDE + z)}

    def along2(d):
        there = (pos2 + d + SIDE) % SIDE
        return {"ctx": jnp.where(r == 0, there * SIDE + z, y * SIDE + there)}

    def per_row(body):
        for rr in range(2):
            pl.when(r == rr)(functools.partial(body, rr))

    ids = {}

    def copy(name, src, dst, device):
        index = ids.setdefault(name, len(ids))
        return pltpu.make_async_remote_copy(
            src_ref=src,
            dst_ref=dst,
            send_sem=send.at[index],
            recv_sem=recv.at[index],
            device_id=device,
            device_id_type=pl.DeviceIdType.MESH,
        )

    class Weights:
        def __init__(self, name, bufs):
            self.name, self.bufs = name, bufs

        def slot(self, rr, away):
            i = (away + REACH + SIDE) % SIDE
            return self.bufs[rr].at[y, i] if rr == 0 else self.bufs[rr].at[i, z]

        def unit(self, rr, away, sub=None):
            i = (pos2 + away + SIDE) % SIDE
            if sub is None:
                return self.bufs[rr].at[i] if rr == 0 else self.bufs[rr].at[:, i]
            cut = pl.ds(sub * (2 * REACH + 1), (2 * REACH + 1, SIDE - 2 * REACH - 1)[sub])
            return self.bufs[rr].at[i, cut] if rr == 0 else self.bufs[rr].at[cut, i]

        def first(self, rr, move, arriving):
            d, away = move
            return copy(
                (self.name, "first", move),
                self.slot(rr, away - d if arriving else away),
                self.slot(rr, away - d),
                along1(d),
            )

        def first_begin(self, rr, moves):
            for move in moves:
                self.first(rr, move, False).start()

        def first_end(self, rr, moves):
            for move in reversed(moves):
                self.first(rr, move, True).wait_recv()

        def second(self, rr, move, arriving):
            d, away, sub = move
            ref = self.unit(rr, away - d if arriving else away, sub)
            return copy((self.name, "second", move), ref, ref, along2(d))

        def to_sibling(self, rr, away, sub=None):
            ref = self.unit(rr, away, sub)
            return copy((self.name, "sibling", away, sub), ref, ref, sibling)

        def pass_on(self, rr, move):
            d, away, sub = move
            self.to_sibling(rr, away - d, sub).start()

        def from_sibling(self, rr):
            self.to_sibling(1 - rr, 0).wait_recv()
            for d, away, sub in self.moves:
                self.to_sibling(1 - rr, away - d, sub).wait_recv()

        def finish(self, rr):
            for move in self.near + self.far:
                self.first(rr, move, False).wait_send()
            self.to_sibling(rr, 0).wait_send()
            for move in self.moves:
                self.second(rr, move, False).wait_send()
                self.to_sibling(rr, move[1] - move[0], move[2]).wait_send()

    kv, query = Weights("kv", (wkb, wvb)), Weights("q", (wq0, wq1))
    kv.near = [(2, 0), (-2, 0), (1, 0), (-1, 0)]
    kv.far = [(4, 0), (3, 0), (-3, 0)]
    query.near, query.far = [(2, 0), (-2, 0), (1, 0), (-1, 0)], [(2, -2), (1, -2), (-1, 2)]
    kv.one = [[(d, 0, sub) for d in (2, -2, 1, -1)] for sub in (0, 1)]
    kv.two = [
        [(1, -2, 0), (-1, 2, 0), (-2, 2, 0)],
        [(1, -2, 1), (-1, 2, 1), (2, -2, 1)],
    ]
    kv.moves = kv.one[0] + kv.one[1] + kv.two[0] + kv.two[1]

    def query_move(way, step, sub):
        return (way, -way * (step - 1), sub)

    query.steps = [(w, s, b) for s in (1, 2, 3) for b in (0, 1) for w in (1, -1)]
    query.steps += [(-1, SIDE // 2, 0), (1, SIDE // 2, 1)]
    query.moves = [query_move(*step) for step in query.steps]

    def query_begin(rr, sub):
        for way in (1, -1):
            query.second(rr, query_move(way, 1, sub), False).start()

    def query_step(rr, step, sub):
        for way in (1, -1):
            if (way, step, sub) in query.steps:
                query.second(rr, query_move(way, step, sub), True).wait_recv()
                if (way, step + 1, sub) in query.steps:
                    query.second(rr, query_move(way, step + 1, sub), False).start()
                query.pass_on(rr, query_move(way, step, sub))

    barrier = pltpu.get_barrier_semaphore()
    partners = [along1(d) for d in FIRST_ORDER] + [along2(d) for d in (1, -1, 2, -2, 4)]
    partners += [sibling, x_right, x_left, span_next, span_prior]
    for device in partners:
        pl.semaphore_signal(barrier, inc=1, device_id=device, device_id_type=pl.DeviceIdType.MESH)

    own_hidden = pltpu.make_async_copy(hid, hbuf.at[x], lsem.at[0])
    own_hidden.start()
    tables = pltpu.make_async_copy(moving_hbm, moving, lsem.at[3])
    tables.start()
    small = [
        pltpu.make_async_copy(src, dst, lsem.at[4 + i])
        for i, (src, dst) in enumerate(
            (
                (published_hbm, published),
                (vertical_hbm, vertical),
                (vcount_hbm, vcount),
                (slash_hbm, slash),
                (scount_hbm, scount),
                (bq_hbm, bq),
                (bk_hbm, bk),
                (bv_hbm, bv),
                (fixed_hbm, fixed),
            )
        )
    ]
    for one in small:
        one.start()

    def own_weights(rr):
        columns = pl.ds(0, left_cols) if rr == 0 else pl.ds(left_cols, wq.shape[1] - left_cols)
        return (
            pltpu.make_async_copy((wk, wv)[rr], kv.slot(rr, 0), lsem.at[1]),
            pltpu.make_async_copy(wq.at[:, columns], query.slot(rr, 0), lsem.at[2]),
        )

    per_row(lambda rr: [one.start() for one in own_weights(rr)] and None)

    pl.semaphore_wait(barrier, len(partners))

    def weights_begin(rr):
        first, second = own_weights(rr)
        first.wait()
        kv.first_begin(rr, kv.near + kv.far)
        second.wait()
        query.first_begin(rr, query.near)

    per_row(weights_begin)

    half = tokens // 2

    def feature(way, sub, far, arriving):
        away = way * ((2 if far else 1) if arriving else (1 if far else 0))
        ref = hbuf.at[(x - away + heads) % heads, pl.ds(sub * half, half)]
        return copy(("x", way, sub, far), ref, ref, x_right if way == 1 else x_left)

    own_hidden.wait()
    for way, sub in ((1, 0), (-1, 1), (1, 1), (-1, 0)):
        feature(way, sub, False, False).start()

    list_sends = [copy(("list", d), vertical_hbm.at[0], lists.at[i], along2(d)) for i, d in ((0, -1), (1, 1))]
    for one in list_sends:
        one.start()

    for one in small:
        one.wait()
    tables.wait()

    rows = lax.broadcasted_iota(jnp.int32, (tokens, tokens), 0)
    columns = lax.broadcasted_iota(jnp.int32, (tokens, tokens), 1)
    bias_local[...] = jnp.where(rows >= columns, 0.0, MASKED)
    back = rows - columns + tokens
    near = jnp.full((tokens, tokens), MASKED, F32)
    for e in range(slash.shape[-1]):
        offset = jnp.where((e < scount[0, 0]) & (c > 0), slash[0, 0, e], 0)
        near = jnp.where(back == offset, 0.0, near)
    bias_near[...] = near

    def kv_send(rr, moves):
        for move in moves:
            kv.second(rr, move, False).start()

    def kv_take(rr, moves):
        for move in moves:
            kv.second(rr, move, True).wait_recv()

    def kv_first(rr):
        kv.first_end(rr, kv.near)
        kv_send(rr, kv.one[0])
        kv.first_end(rr, kv.far)
        kv_send(rr, kv.one[1])
        query.first_end(rr, query.near)
        query.first_begin(rr, query.far)
        query_begin(rr, 0)
        kv.to_sibling(rr, 0).start()

    per_row(kv_first)
    for way, sub in ((1, 0), (-1, 1)):
        feature(way, sub, False, True).wait_recv()
        feature(way, sub, True, False).start()

    def spread(rr):
        for sub in (0, 1):
            kv_take(rr, kv.one[sub])
            kv_send(rr, kv.two[sub])
        for move in kv.one[0] + kv.one[1]:
            kv.pass_on(rr, move)
        query.first_end(rr, query.far)
        query_begin(rr, 1)
        query.to_sibling(rr, 0).start()
        query_step(rr, 1, 0)
        for sub in (0, 1):
            kv_take(rr, kv.two[sub])
            for move in kv.two[sub]:
                kv.pass_on(rr, move)
        query_step(rr, 1, 1)
        kv.from_sibling(rr)

    per_row(spread)
    for way, sub in ((1, 1), (-1, 0)):
        feature(way, sub, False, True).wait_recv()
    for way, sub in ((1, 0), (-1, 1)):
        feature(way, sub, True, True).wait_recv()

    def gathered(h, rr, one):
        def rank(i, pos):
            return (i - pos + REACH + SIDE) % SIDE

        down, across = [2 * h, 2 * h + 1], range(SIDE)
        if rr == 0:
            across = [rank(i, z) for i in across]
        else:
            down = [rank(i, y) for i in down]
        return jnp.concatenate([one[i, j] for i in down for j in across], axis=0)

    def project(h, *weights):
        block = jnp.concatenate([gathered(h, rr, one) for rr, one in weights], axis=1)
        return jnp.dot(hbuf[h], block, preferred_element_type=F32)

    def project_all(*weights):
        total = project(0, *weights)
        for h in range(1, heads):
            total = total + project(h, *weights)
        return total

    def query_steps(*steps):
        per_row(lambda rr: [query_step(rr, *one) for one in steps] and None)

    both = project_all((0, wkb), (1, wvb))
    keys = rotate(both[:, :width] + bk[...][None, :], moving[0], moving[1]).astype(BF16)
    kt[0] = keys.T
    vv[0] = (both[:, width:] + bv[...][None, :]).astype(BF16)

    here = pool.at[pos1, pos2 // 2]
    first_block = published[0, 0] == 0
    here[0] = jnp.where(first_block, kt[0, :, :BLOCK], kt[0, :, BLOCK:])
    here[1] = jnp.where(first_block, vv[0, :BLOCK], vv[0, BLOCK:])

    def alike(d, arriving):
        place = (pos2 - d + SIDE) % SIDE if arriving else pos2
        ref = pool.at[pos1, place // 2]
        return copy(("alike", d), ref, ref, along2(d))

    offsets = (0, 2, -2, 4)

    def around(way, step, o, arriving):
        i = (pos1 - way * (step if arriving else step - 1) + SIDE) % SIDE
        ref = pool.at[i, (pos2 + o + SIDE) % SIDE // 2]
        return copy(("round", way, step, o), ref, ref, along1(way))

    def ways(step, o):
        return (1, -1) if step < SIDE // 2 else (-1,)

    def round_begin(o):
        for way in (1, -1):
            around(way, 1, o, False).start()

    def round_step(step, o):
        for way in ways(step, o):
            around(way, step, o, True).wait_recv()
            if step < SIDE // 2 and way in ways(step + 1, o):
                around(way, step + 1, o, False).start()

    for d in (2, -2, 4):
        alike(d, False).start()
    round_begin(0)
    query_steps((2, 0), (2, 1))
    round_step(1, 0)
    for d in (2, -2):
        alike(d, True).wait_recv()
        round_begin(-d)
    for way, sub in ((1, 0), (-1, 1), (1, 1), (-1, 0)):
        feature(way, sub, False, False).wait_send()
    for way, sub in ((1, 0), (-1, 1)):
        feature(way, sub, True, False).wait_send()
    per_row(kv.finish)
    alike(4, True).wait_recv()
    round_begin(4)
    round_step(2, 0)
    round_step(1, 2)
    round_step(1, -2)
    query_steps((3, 0))
    round_step(1, 4)
    query_steps((3, 1))
    behind = [
        copy(("prior", "k"), kt.at[0], kt.at[1], span_next),
        copy(("prior", "v"), vv.at[0], vv.at[1], span_next),
    ]
    for one in behind:
        one.start()
    round_step(3, 0)
    round_step(2, 2)
    round_step(2, -2)

    def last_steps(rr):
        for sub in (0, 1):
            query_step(rr, SIDE // 2, sub)

    per_row(lambda rr: query.from_sibling(rr) if rr else last_steps(rr))

    def rotate_head(g):
        columns = pl.ds(pl.multiple_of(g * width, width), width)
        raw = qraw[:, columns] + bq[columns][None, :]
        swapped = pltpu.roll(raw, width // 2, axis=1)
        ql[g] = (raw * moving[0] + swapped * moving[1]).astype(BF16)
        qn[g] = (raw * moving[2] + swapped * moving[3]).astype(BF16)
        qf[g] = (raw * fixed[0:1] + swapped * fixed[1:2]).astype(BF16)

    left_heads = left_cols // width
    qraw[:, :left_cols] = project_all((0, wq0))
    round_step(2, 4)
    round_step(4, 0)
    round_step(3, 2)
    round_step(3, -2)
    pl.loop(0, left_heads)(rotate_head)
    per_row(lambda rr: last_steps(rr) if rr else query.from_sibling(rr))
    round_step(3, 4)
    qraw[:, left_cols:] = project_all((1, wq1))
    round_step(4, 2)
    round_step(4, -2)
    pl.loop(left_heads, group, unroll=True)(rotate_head)
    for one in behind:
        one.wait_recv()

    def close_part(g):
        local = jnp.dot(ql[g], kt[0], preferred_element_type=F32) * score_scale + bias_local[...]
        slashed = jnp.dot(qn[g], kt[1], preferred_element_type=F32) * score_scale + bias_near[...]
        highest = jnp.maximum(
            jnp.max(local, axis=1, keepdims=True), jnp.max(slashed, axis=1, keepdims=True)
        )
        local, slashed = jnp.exp2(local - highest), jnp.exp2(slashed - highest)
        total = jnp.sum(local, axis=1, keepdims=True) + jnp.sum(slashed, axis=1, keepdims=True)
        top1[g] = jnp.broadcast_to(highest, (tokens, width))
        sum1[g] = jnp.broadcast_to(total, (tokens, width))
        acc1[g] = jnp.dot(local.astype(BF16), vv[0], preferred_element_type=F32) + jnp.dot(
            slashed.astype(BF16), vv[1], preferred_element_type=F32
        )

    pl.loop(0, 1)(close_part)
    round_step(4, 4)

    def place_of(span):
        across, down = span % SIDE, span // SIDE
        return jnp.where(r == 0, across, down), jnp.where(r == 0, down, across)

    for one in list_sends:
        one.wait_recv()
    each = slots // 2
    trades = {}
    for which in range(2):
        for side, d in ((0, 1), (1, -1)):
            for e in range(each):
                one, two = place_of(lists[side, 0, side * each + e])
                chosen[side, which, e] = pool[one, two // 2, which]
            src, dst = chosen.at[side, which], got.at[side, which]
            trades[side, which] = copy(("trade", d, which), src, dst, along2(d))
            trades[side, which].start()
    pl.loop(1, group, unroll=True)(close_part)

    def listed(e, which):
        one, two = place_of(vertical[0, 0, e])
        traded = got[e // each, which, e % each]
        return jnp.where(two % 2 == pos2 % 2, pool[one, two // 2, which], traded)

    per_row(query.finish)
    for d in (4, 2, -2):
        alike(d, False).wait_send()
    for o in offsets:
        for step in (1, 2, 3, 4):
            for way in ways(step, o):
                around(way, step, o, False).wait_send()
    for one in behind + list_sends:
        one.wait_send()
    for side in range(2):
        trades[side, 0].wait_recv()
    for e in range(slots):
        kft[:, e * BLOCK : (e + 1) * BLOCK] = listed(e, 0)
    place = lax.broadcasted_iota(jnp.int32, (1, slots * BLOCK), 1)
    bias_far = jnp.where(place < vcount[0, 0] * BLOCK, 0.0, MASKED)

    def far_scores(g):
        return jnp.dot(qf[g], kft[...], preferred_element_type=F32) * score_scale + bias_far

    def far_part(g, scores):
        before = top1[g][:, :1]
        highest = jnp.maximum(before, jnp.max(scores, axis=1, keepdims=True))
        weights = jnp.exp2(scores - highest)
        fade = jnp.exp2(before - highest)
        total = sum1[g][:, :1] * fade + jnp.sum(weights, axis=1, keepdims=True)
        combined = acc1[g] * fade + jnp.dot(
            weights.astype(BF16), vft[...], preferred_element_type=F32
        )
        columns = pl.ds(g * width, width)
        out[:, columns] = (combined / total).astype(BF16)

    scores = far_scores(0)
    for side in range(2):
        trades[side, 1].wait_recv()
    for e in range(slots):
        vft[e * BLOCK : (e + 1) * BLOCK] = listed(e, 1)
    for g in range(group):
        following = far_scores(g + 1) if g + 1 < group else None
        far_part(g, scores)
        scores = following

    for one in trades.values():
        one.wait_send()


def on_device(
    hidden_states, w_query, key_weight_matrix, value_weight_matrix, bias_query, bias_key,
    value_bias_vector, published, vertical, vcount, slash_offsets, scount,
):
    tokens, part = hidden_states.shape
    depth, width = key_weight_matrix.shape
    columns = w_query.shape[1]
    group = columns // width
    heads = lax.axis_size("head")
    slots = vertical.shape[-1]
    left = (group // 2) * width
    moving, fixed = rope_tables(tokens, width)
    hbm = pl.BlockSpec(memory_space=pl.ANY)
    copies = 160
    return pl.pallas_call(
        kernel,
        out_shape=pltpu.VMEM((tokens, columns), BF16),
        in_specs=[hbm] * 14,
        out_specs=pl.BlockSpec(memory_space=pltpu.VMEM),
        scratch_shapes=[
            pltpu.VMEM(bias_query.shape, F32),
            pltpu.VMEM(bias_key.shape, F32),
            pltpu.VMEM(value_bias_vector.shape, F32),
            pltpu.VMEM(fixed.shape, F32),
            pltpu.VMEM(moving.shape, F32),
            pltpu.SMEM(published.shape, jnp.int32),
            pltpu.SMEM(vertical.shape, jnp.int32),
            pltpu.SMEM(vcount.shape, jnp.int32),
            pltpu.SMEM(slash_offsets.shape, jnp.int32),
            pltpu.SMEM(scount.shape, jnp.int32),
            pltpu.VMEM((heads, tokens, part), BF16),
            pltpu.VMEM((SIDE, SIDE, depth, width), BF16),
            pltpu.VMEM((SIDE, SIDE, depth, width), BF16),
            pltpu.VMEM((SIDE, SIDE, depth, left), BF16),
            pltpu.VMEM((SIDE, SIDE, depth, columns - left), BF16),
            pltpu.VMEM((SIDE, SIDE // 2, 2, BLOCK, width), BF16),
            pltpu.VMEM((2, 2, slots // 2, BLOCK, width), BF16),
            pltpu.VMEM((2, 2, slots // 2, BLOCK, width), BF16),
            pltpu.SMEM((2, 1, slots), jnp.int32),
            pltpu.VMEM((2, width, tokens), BF16),
            pltpu.VMEM((2, tokens, width), BF16),
            pltpu.VMEM((tokens, columns), F32),
            pltpu.VMEM((group, tokens, width), BF16),
            pltpu.VMEM((group, tokens, width), BF16),
            pltpu.VMEM((group, tokens, width), BF16),
            pltpu.VMEM((width, slots * BLOCK), BF16),
            pltpu.VMEM((slots * BLOCK, width), BF16),
            pltpu.VMEM((group, tokens, width), F32),
            pltpu.VMEM((group, tokens, width), F32),
            pltpu.VMEM((group, tokens, width), F32),
            pltpu.VMEM((tokens, tokens), F32),
            pltpu.VMEM((tokens, tokens), F32),
            pltpu.SemaphoreType.DMA((copies,)),
            pltpu.SemaphoreType.DMA((copies,)),
            pltpu.SemaphoreType.DMA((13,)),
            pltpu.SemaphoreType.DMA((group,)),
        ],
        compiler_params=pltpu.CompilerParams(
            collective_id=0, has_side_effects=True, vmem_limit_bytes=56 * 1024 * 1024
        ),
        cost_estimate=pl.CostEstimate(
            flops=4 * 10**9, bytes_accessed=10**7, transcendentals=3 * 10**6
        ),
    )(
        hidden_states, key_weight_matrix, value_weight_matrix, w_query, jnp.asarray(moving),
        published, vertical, vcount, slash_offsets, scount,
        bias_query, bias_key, value_bias_vector, jnp.asarray(fixed),
    )


def solution(mesh):
    spans, kept = P(("row", "ctx"), "head"), P(("row", "ctx"), "head", None)
    weight, bias = P("ctx", "head"), P("head")
    return jax.shard_map(
        on_device,
        mesh=mesh,
        in_specs=(spans, weight, weight, weight, bias, bias, bias, spans, kept, spans, kept, spans),
        out_specs=spans,
        check_vma=False,
    )
```
